32 devices in a mesh: net: 8 (over z, y), hour: 4 (over x, core).
Axes of the slice: x: 2, y: 2, z: 4, core: 2. Of those that a mesh axis runs over, the one named last changes fastest.
Arguments:
- measured: float32 [1024, 2048], P('net', 'hour')
- prior_flow: float32 [1024, 2048], P('net', 'hour'), may hold values from -6 to 6
- demand: float32 [768, 2048], P('net', 'hour'), may hold values from -6 to 6
- pipe_sigma: float32 [1024], P('net'), may hold values from 0.5 to 2
- whiten_coef: float32 [512], replicated
- pipe_tail: int32 [1024], P('net'), may hold values from 0 to 95
- pipe_head: int32 [1024], P('net'), may hold values from 0 to 95
- boundary_pipe: int32 [8, 2, 8], P('net'), may hold values from 0 to 127, as said below
- boundary_count: int32 [8, 2], P('net'), may hold values from 0 to 8, as said below
- arrival_junction: int32 [8, 2, 8], P('net'), may hold values from 0 to 95
Outputs:
- flows: float32 [1024, 2048], P('net', 'hour')
- residual: float32 [1024, 2048], P('net', 'hour')
The draws below stay inside these ranges and needn't reach their ends.
Inputs may be any that keep to these rules, and one draw needn't show every extreme that they name: `boundary_pipe`: the 16 entries of one partition's two lists are distinct local pipe numbers. `boundary_count`: partition 0 has no live slot toward side 0 and partition 8 - 1 none toward side 1.
All inputs are finite; a program needn't handle non-finite values.
Results may differ from the reference program's by a relative error of at most 0.00026.
Values sent between devices are 32-bit elements; how exact they have to be, the bound alone decides.
A program may use at most 64 MiB of HBM per device.

```python
import math
import jax
import jax.numpy as jnp
from jax import lax

P_DEV = 128
BLK = 512
ITERS = 3
J_DEV = 96
CAP = 8
NETS = 8
PIPES = 1024
JUNCS = 768
HOURS = 2048
N_HOUR = 4


def draw_measured(key, part):
    first_key = jax.random.fold_in(key, 0)
    row_pos = jnp.arange(PIPES, dtype=jnp.float32)[:, None]
    trend = 1.0 + 2.0 * row_pos / (PIPES - 1)
    base = jnp.clip(jax.random.normal(first_key, (PIPES, HOURS), jnp.float32), -6.0, 6.0)
    return (base * trend).astype(jnp.float32)


def draw_whiten_coef(key, part):
    lead_key, tap_key = jax.random.split(key)
    lags = jnp.arange(BLK, dtype=jnp.float32)
    ratio = 1.0 - 4.0 / BLK
    decay = 0.6 * (4.0 / BLK) * jnp.exp((lags - 1.0) * math.log(ratio))
    taps = jax.random.uniform(tap_key, (BLK,), jnp.float32, -1.0, 1.0)
    lead = jax.random.uniform(lead_key, (), jnp.float32, 0.8, 1.2)
    return jnp.where(lags == 0.0, lead, taps * decay).astype(jnp.float32)


def draw_boundary_pipe(key, part):
    keys = jax.random.split(key, NETS)

    def one_partition(sub_key):
        order = jax.random.permutation(sub_key, P_DEV)
        return order[:2 * CAP].reshape(2, CAP)
    return jax.vmap(one_partition)(keys).astype(jnp.int32)


def draw_boundary_count(key, part):
    count_key, full_key = jax.random.split(key)
    counts = jax.random.randint(count_key, (NETS, 2), CAP // 4, CAP + 1).astype(jnp.int32)
    full_row = jax.random.randint(full_key, (), 0, NETS - 1).astype(jnp.int32)
    partitions = jnp.arange(NETS, dtype=jnp.int32)
    upper_side = jnp.where(partitions == full_row, CAP, counts[:, 1])
    counts = jnp.stack([counts[:, 0], upper_side], axis=1)
    counts = counts.at[0, 0].set(0)
    counts = counts.at[NETS - 1, 1].set(0)
    return counts.astype(jnp.int32)


def plant(values, stream_key, smallest, top_value):
    extent = values.shape
    index_at = [jax.random.randint(jax.random.fold_in(stream_key, axis), (), 0, extent[axis]) for axis in range(len(extent))]
    values = values.at[tuple(index_at)].set(smallest)
    longest = extent.index(max(extent))
    index_at[longest] = (index_at[longest] + 1) % extent[longest]
    return values.at[tuple(index_at)].set(top_value)


def level_of(rng, dims, cuts, smallest, largest):
    def one(dim, parts):
        heights = jax.random.uniform(jax.random.fold_in(jax.random.fold_in(rng, 6), dim), (parts,), jnp.float32, smallest / len(cuts), largest / len(cuts))
        return jnp.repeat(jnp.exp(heights), dims[dim] // parts).reshape((-1,) + (1,) * (len(dims) - dim - 1))

    gain = one(*cuts[0])
    for cut in cuts[1:]:
        gain = gain * one(*cut)
    return gain


def scatter_about(own_key, dims, spread, most, cuts=(), held_as=jnp.bfloat16):
    entries = jax.random.normal(own_key, dims, jnp.float32) * spread
    if len(cuts) > 0:
        entries = level_of(own_key, dims, cuts, -0.22, 0.18) * entries
    return jnp.clip(entries, min=-most, max=most).astype(held_as)


def setup_inputs(seed: int = 0) -> dict:
    streams_of = jax.random.split(jax.random.key(seed), 11)
    measured = draw_measured(jax.random.fold_in(streams_of[10], 71), 0)
    prior_flow = scatter_about(streams_of[1], (PIPES, HOURS), 1.0, 6.0, ((0, 8), (1, 4)), jnp.float32)
    demand = scatter_about(streams_of[2], (JUNCS, HOURS), 1.0, 6.0, ((0, 8), (1, 4)), jnp.float32)
    pipe_sigma = jnp.clip(jnp.exp(math.log(2.0) - 1.3862944 * jax.random.uniform(streams_of[3], (PIPES,), jnp.float32) ** level_of(streams_of[3], (PIPES,), ((0, 8),), -0.2, 0.2)), 0.5, 2.0)
    whiten_coef = draw_whiten_coef(jax.random.fold_in(streams_of[10], 71), 0)
    pipe_tail = plant(jax.random.randint(streams_of[5], (PIPES,), 0, J_DEV), jax.random.fold_in(streams_of[5], 1), 0, J_DEV - 1).astype(jnp.int32)
    pipe_head = plant(jax.random.randint(streams_of[6], (PIPES,), 0, J_DEV), jax.random.fold_in(streams_of[6], 1), 0, J_DEV - 1).astype(jnp.int32)
    boundary_pipe = draw_boundary_pipe(jax.random.fold_in(streams_of[10], 71), 0)
    boundary_count = draw_boundary_count(jax.random.fold_in(streams_of[10], 71), 0)
    arrival_junction = plant(jax.random.randint(streams_of[9], (NETS, 2, CAP), 0, J_DEV), jax.random.fold_in(streams_of[9], 1), 0, J_DEV - 1).astype(jnp.int32)
    return {"measured": measured, "prior_flow": prior_flow, "demand": demand, "pipe_sigma": pipe_sigma, "whiten_coef": whiten_coef, "pipe_tail": pipe_tail, "pipe_head": pipe_head, "boundary_pipe": boundary_pipe, "boundary_count": boundary_count, "arrival_junction": arrival_junction}


huber_edge = 1.5
penalty = 4.0


def whiten_matrix(whiten_coef):
    length = whiten_coef.shape[0]
    positions = jnp.arange(length, dtype=jnp.int32)
    lag_index = positions[:, None] - positions[None, :]
    taps = whiten_coef[jnp.clip(lag_index, 0, length - 1)]
    return jnp.where(lag_index >= 0, taps, jnp.zeros_like(taps))


def reference(measured, prior_flow, demand, pipe_sigma, whiten_coef, pipe_tail, pipe_head, boundary_pipe, boundary_count, arrival_junction):
    whitener = whiten_matrix(whiten_coef)

    def forward_filter(field):
        blocks = field.reshape(PIPES, N_HOUR, BLK)
        out = jnp.einsum("pnb,cb->pnc", blocks, whitener, precision=lax.Precision.HIGHEST)
        return out.reshape(PIPES, HOURS)

    def backward_filter(field):
        blocks = field.reshape(PIPES, N_HOUR, BLK)
        out = jnp.einsum("pnc,cb->pnb", blocks, whitener, precision=lax.Precision.HIGHEST)
        return out.reshape(PIPES, HOURS)

    variance = (pipe_sigma * pipe_sigma)[:, None]
    whitened = forward_filter((measured - prior_flow) / pipe_sigma[:, None])
    huber_weight = huber_edge / jnp.maximum(jnp.abs(whitened), huber_edge)

    def quadratic(field):
        return backward_filter(huber_weight * forward_filter(field)) / variance

    pipe_ids = jnp.arange(PIPES, dtype=jnp.int32)
    owner = pipe_ids // P_DEV
    tail_global = owner * J_DEV + pipe_tail
    head_global = owner * J_DEV + pipe_head
    slot_ids = jnp.arange(CAP, dtype=jnp.int32)
    live_mask = (slot_ids[None, None, :] < boundary_count[:, :, None]).astype(jnp.float32)
    partitions = jnp.arange(NETS, dtype=jnp.int32)
    source_global = partitions[:, None, None] * P_DEV + boundary_pipe
    below_junction = jnp.roll(arrival_junction[:, 1, :], 1, axis=0)
    above_junction = jnp.roll(arrival_junction[:, 0, :], -1, axis=0)
    dest_below = (partitions[:, None] - 1) * J_DEV + below_junction
    dest_above = (partitions[:, None] + 1) * J_DEV + above_junction
    dest_global = jnp.clip(jnp.stack([dest_below, dest_above], axis=1), 0, JUNCS - 1).astype(jnp.int32)
    source_flat = source_global.reshape(-1)
    dest_flat = dest_global.reshape(-1)
    live_flat = live_mask.reshape(-1)
    interior = (1.0 - jnp.zeros((PIPES,), jnp.float32).at[source_flat].add(live_flat))[:, None]
    live_rows = live_flat[:, None]

    def balance_of(field):
        heads = jnp.zeros((JUNCS, HOURS), jnp.float32).at[head_global].add(field * interior)
        tails = jnp.zeros((JUNCS, HOURS), jnp.float32).at[tail_global].add(field)
        remote = jnp.zeros((JUNCS, HOURS), jnp.float32).at[dest_flat].add(field[source_flat] * live_rows)
        return heads - tails + remote

    def adjoint_of(balance):
        remote = jnp.zeros((PIPES, HOURS), jnp.float32).at[source_flat].add(balance[dest_flat] * live_rows)
        return balance[head_global] * interior - balance[tail_global] + remote

    def operator(field):
        return quadratic(field) + penalty * adjoint_of(balance_of(field))

    rhs = quadratic(measured) + penalty * adjoint_of(demand)
    flows = prior_flow
    residual = rhs - operator(flows)
    direction = residual
    norm_now = jnp.sum(residual * residual)
    for iteration in range(ITERS):
        image = operator(direction)
        step_size = norm_now / jnp.sum(direction * image)
        flows = flows + step_size * direction
        residual = residual - step_size * image
        norm_next = jnp.sum(residual * residual)
        direction = residual + (norm_next / norm_now) * direction
        norm_now = norm_next
    return flows, residual
```

```python
import functools

import jax
import jax.numpy as jnp
from jax import lax
from jax.experimental import pallas as pl
from jax.experimental.pallas import tpu as pltpu
from jax.sharding import PartitionSpec as P

ITERS = 3
EDGE = 1.5
PENALTY = 4.0
MESH = pl.DeviceIdType.MESH
f32 = jnp.float32
bf16 = jnp.bfloat16


def dot(a, b):
    return jnp.dot(a, b, preferred_element_type=f32)


def split2(x):
    high = x.astype(bf16)
    return high, (x - high.astype(f32)).astype(bf16)


def split3(x):
    high = x.astype(bf16)
    rest = x - high.astype(f32)
    mid = rest.astype(bf16)
    return high, mid, (rest - mid.astype(f32)).astype(bf16)


def total(x):
    return jnp.sum(jnp.sum(x, axis=0, keepdims=True), axis=1, keepdims=True)


def halves(x):
    half = x.shape[1] // 2
    return jnp.concatenate([x[:, :half], x[:, half:]], axis=0)


def joined(x):
    half = x.shape[0] // 2
    return jnp.concatenate([x[:half], x[half:]], axis=1)


def kernel(
    nets,
    hours,
    measured_ref,
    prior_ref,
    demand_ref,
    sigma_ref,
    coef_ref,
    tail_ref,
    head_ref,
    pipe_ref,
    count_ref,
    arrival_ref,
    flows_ref,
    residual_ref,
    basis,
    weight,
    toep,
    outgoing,
    incoming,
    pairs_out,
    pairs_in,
    part,
    parts,
    row_send,
    row_recv,
    pair_send,
    pair_recv,
    sum_send,
    sum_recv,
):
    pipes, length = prior_ref.shape
    juncs = demand_ref.shape[0]
    cap = pipe_ref.shape[2]
    half = length // 2
    net = lax.axis_index("net")
    hour = lax.axis_index("hour")
    everyone = nets * hours
    me = net * hours + hour
    has_left, has_right = net > 0, net < nets - 1
    has_left2, has_right2 = net > 1, net < nets - 2

    def clear(missing, ref):
        @pl.when(missing)
        def _():
            ref[...] = jnp.zeros(ref.shape, f32)

    for r in range(ITERS + 1):
        clear(net == 0, incoming.at[r, pl.ds(0, 2 * cap)])
        clear(net == nets - 1, incoming.at[r, pl.ds(2 * cap, 2 * cap)])
        clear(net < 2, incoming.at[r, pl.ds(4 * cap, cap)])
        clear(net >= nets - 2, incoming.at[r, pl.ds(5 * cap, cap)])
    clear(net == 0, pairs_in.at[0])
    clear(net == nets - 1, pairs_in.at[1])

    barrier = pltpu.get_barrier_semaphore()

    def greet(i, carry):
        peer = lax.rem(me + i, everyone)
        pl.semaphore_signal(
            barrier,
            inc=1,
            device_id=(peer // hours, lax.rem(peer, hours)),
            device_id_type=MESH,
        )
        return carry

    lax.fori_loop(1, everyone, greet, 0)

    slots = 4 * cap
    sub = lax.broadcasted_iota(jnp.int32, (slots, pipes), 0)
    lane = lax.broadcasted_iota(jnp.int32, (slots, pipes), 1)
    target = jnp.full((slots, pipes), -1, jnp.int32)
    for s in range(2):
        live = count_ref[0, s]
        for k in range(cap):
            own = jnp.where(k < live, pipe_ref[0, s, k], -1)
            target = jnp.where(sub == 2 * s * cap + k, own, target)
    chosen = (lane == target).astype(f32)
    sub_j = lax.broadcasted_iota(jnp.int32, (slots, juncs), 0)
    lane_j = lax.broadcasted_iota(jnp.int32, (slots, juncs), 1)
    landing_at = jnp.full((slots, juncs), -1, jnp.int32)
    for s in range(2):
        for k in range(cap):
            landing_at = jnp.where(
                sub_j == (2 * s + 1) * cap + k, arrival_ref[0, s, k], landing_at
            )
    landing = (lane_j == landing_at).astype(f32)
    interior = 1.0 - jnp.sum(chosen, axis=0, keepdims=True)
    junction = lax.broadcasted_iota(jnp.int32, (juncs, pipes), 0)
    incidence = (junction == head_ref[...]).astype(f32) * interior - (
        junction == tail_ref[...]
    ).astype(f32)
    landing16 = landing.astype(bf16)
    reach = chosen + dot(landing16, incidence.astype(bf16))

    def swapped(x):
        return jnp.concatenate(
            [
                x[cap : 2 * cap],
                x[:cap],
                x[3 * cap :],
                x[2 * cap : 3 * cap],
            ],
            axis=0,
        )

    reach_out = swapped(reach).astype(bf16)
    reach_out3 = jnp.concatenate([reach_out] * 3, axis=1)
    landing_out = swapped(landing).astype(bf16)
    pad_l = jnp.concatenate([landing, jnp.zeros((128 - slots, juncs), f32)], axis=0)
    pairs_out[...] = lax.dot_general(
        landing16,
        pad_l.astype(bf16),
        (((1,), (1,)), ((), ())),
        preferred_element_type=f32,
    )

    pl.semaphore_wait(barrier, everyone - 1)

    def remote(src, dst, send, recv, shift):
        return pltpu.make_async_remote_copy(
            src_ref=src,
            dst_ref=dst,
            send_sem=send,
            recv_sem=recv,
            device_id=(net + shift, hour),
            device_id_type=MESH,
        )

    def pair_copies():
        yield has_right, has_left, remote(
            pairs_out, pairs_in.at[0], pair_send.at[0], pair_recv.at[0], 1
        )
        yield has_left, has_right, remote(
            pairs_out, pairs_in.at[1], pair_send.at[1], pair_recv.at[1], -1
        )

    def row_copies(r):
        def one(i, start, size, dest, shift):
            return remote(
                outgoing.at[r, pl.ds(start, size)],
                incoming.at[r, pl.ds(dest, size)],
                row_send.at[r, i],
                row_recv.at[r, i],
                shift,
            )

        yield has_right, has_left, one(0, 2 * cap, 2 * cap, 0, 1)
        yield has_left, has_right, one(1, 0, 2 * cap, 2 * cap, -1)
        yield has_right2, has_left2, one(2, 3 * cap, cap, 4 * cap, 2)
        yield has_left2, has_right2, one(3, cap, cap, 5 * cap, -2)

    def start(copies):
        for sends, _, copy in copies:

            @pl.when(sends)
            def _():
                copy.start()

    def arrived(copies):
        for _, receives, copy in copies:

            @pl.when(receives)
            def _():
                copy.wait_recv()

    def left_here(copies):
        for sends, _, copy in copies:

            @pl.when(sends)
            def _():
                copy.wait_send()

    prior = prior_ref[...]
    prior_cut = jnp.concatenate(split3(prior), axis=0)
    wanted = jnp.concatenate(split3(demand_ref[...]), axis=0)
    start(pair_copies())
    outgoing[0] = dot(reach_out3, prior_cut) - dot(
        jnp.concatenate([landing_out] * 3, axis=1), wanted
    )
    start(row_copies(0))

    spread = jnp.broadcast_to(coef_ref[...], (half, length))
    rolled = pltpu.roll(spread, 0, 1, stride=1, stride_axis=0)
    at_row = lax.broadcasted_iota(jnp.int32, (half, half), 0)
    at_col = lax.broadcasted_iota(jnp.int32, (half, half), 1)
    near = jnp.where(at_col >= at_row, rolled[:, :half], 0.0)
    far = rolled[:, half:]
    for i, block in enumerate((near, far, near.T, far.T)):
        high, low = split2(block)
        toep[i, 0] = high
        toep[i, 1] = low

    def thrice(high, low, i):
        return (
            dot(high, toep[i, 0]) + dot(low, toep[i, 0]) + dot(high, toep[i, 1])
        )

    def forward(high, low):
        high, low = halves(high), halves(low)
        same = thrice(high, low, 0)
        cross = thrice(high[:pipes], low[:pipes], 1)
        return jnp.concatenate([same[:pipes], same[pipes:] + cross], axis=1)

    def backward(field):
        high, low = split2(halves(field))
        same = thrice(high, low, 2)
        cross = thrice(high[pipes:], low[pipes:], 3)
        return jnp.concatenate([same[:pipes] + cross, same[pipes:]], axis=1)

    eye = lax.broadcasted_iota(jnp.int32, (pipes, pipes), 0) == (
        lax.broadcasted_iota(jnp.int32, (pipes, pipes), 1)
    )
    sigma = jnp.sum(jnp.where(eye, sigma_ref[...], 0.0), axis=1, keepdims=True)
    inverse = 1.0 / sigma
    inverse2 = inverse * inverse
    whitened = forward(*split2((measured_ref[...] - prior) * inverse))
    huber = EDGE / jnp.maximum(jnp.abs(whitened), EDGE)
    weight[...] = huber
    near_part = backward(huber * whitened * sigma) * inverse2

    taps = jnp.sum(jnp.abs(coef_ref[...]), axis=1, keepdims=True)
    scale = 1.0 / (32.0 + 4.0 * taps * taps)

    arrived(pair_copies())
    zero = jnp.zeros((cap, pipes), f32)
    fill = jnp.zeros((128 - slots, pipes), f32)
    lower = chosen[:cap]
    upper = chosen[2 * cap : 3 * cap]
    lower_at = jnp.concatenate([zero, zero, zero, lower, fill], axis=0)
    upper_at = jnp.concatenate([zero, upper, zero, zero, fill], axis=0)
    from_left = dot(pairs_in[0].astype(bf16), lower_at.astype(bf16))
    from_right = dot(pairs_in[1].astype(bf16), upper_at.astype(bf16))
    gather = jnp.concatenate(
        [reach, from_left[cap : 2 * cap], from_right[3 * cap :]], axis=0
    )
    width = 6 * cap
    deep = -(-3 * width // 128) * 128
    gather3 = jnp.concatenate(
        [gather] * 3 + [jnp.zeros((deep - 3 * width, pipes), f32)], axis=0
    )
    spread_in = (PENALTY * gather3.T).astype(bf16)
    tall = -(-(juncs + 2 * cap) // 128) * 128
    rest = jnp.zeros((tall - juncs - 2 * cap, pipes), f32)
    left_side = jnp.concatenate([incidence, lower, upper, rest], axis=0).T
    right_side = jnp.concatenate(
        [incidence, from_left[3 * cap :], from_right[cap : 2 * cap], rest], axis=0
    )
    local = (
        PENALTY * dot(left_side.astype(bf16), right_side.astype(bf16))
    ).astype(bf16)
    local3 = jnp.concatenate([local] * 3, axis=1)
    back = (PENALTY * left_side).astype(bf16)
    empty = jnp.zeros((tall - juncs, length), bf16)
    wanted = jnp.concatenate(
        [
            x
            for i in range(3)
            for x in (wanted[i * juncs : (i + 1) * juncs], empty)
        ],
        axis=0,
    )
    tail_rows = jnp.zeros((deep - 3 * width, length), bf16)

    def received(r):
        arrived(row_copies(r))
        cut = jnp.concatenate(split3(incoming[r]) + (tail_rows,), axis=0)
        return dot(spread_in, cut)

    here = near_part + dot(jnp.concatenate([back] * 3, axis=1), wanted)
    here = here - dot(local3, prior_cut)
    vector = here - received(0)
    basis[0] = vector
    moments = []
    for r in range(1, ITERS + 1):
        pieces = split3(vector)
        cut = jnp.concatenate(pieces, axis=0)
        outgoing[r] = dot(reach_out3, cut)
        start(row_copies(r))
        moments.append(total(vector * vector))
        here = dot(local3, cut)
        filtered = forward(pieces[0], pieces[1])
        here = here + backward(weight[...] * filtered) * inverse2
        after = (here + received(r)) * scale
        moments.append(total(vector * after))
        vector = after
        basis[r] = vector

    at = lax.broadcasted_iota(jnp.int32, (1, 128), 1)
    mine = jnp.zeros((1, 128), f32)
    for i, value in enumerate(moments):
        mine = jnp.where(at == i, value, mine)
    part[...] = mine

    def share(i, carry):
        peer = lax.rem(me + i, everyone)
        pltpu.make_async_remote_copy(
            src_ref=part,
            dst_ref=parts.at[i - 1],
            send_sem=sum_send,
            recv_sem=sum_recv,
            device_id=(peer // hours, lax.rem(peer, hours)),
            device_id_type=MESH,
        ).start()
        return carry

    lax.fori_loop(1, everyone, share, 0)
    for r in range(ITERS + 1):
        left_here(row_copies(r))
    left_here(pair_copies())
    pltpu.make_async_copy(parts, parts, sum_recv).wait()
    sums = mine + jnp.sum(parts[...], axis=0)
    pltpu.make_async_copy(parts, parts, sum_send).wait()
    moment = [sums[:, i : i + 1] for i in range(2 * ITERS)]

    def product(a, b, shift):
        out = None
        for i, x in enumerate(a):
            for j, y in enumerate(b):
                term = x * y * moment[i + j + shift]
                out = term if out is None else out + term
        return out

    def plus(a, factor, b):
        n = max(len(a), len(b))
        none = jnp.zeros((1, 1), f32)
        a = a + [none] * (n - len(a))
        b = b + [none] * (n - len(b))
        return [x + factor * y for x, y in zip(a, b)]

    one = jnp.ones((1, 1), f32)
    remaining, direction, moved = [one], [one], []
    now = moment[0]
    for i in range(ITERS):
        step = now / product(direction, direction, 1)
        moved = plus(moved, step * scale, direction)
        remaining = plus(remaining, -step, [jnp.zeros((1, 1), f32)] + direction)
        if i + 1 < ITERS:
            later = product(remaining, remaining, 0)
            direction = plus(remaining, later / now, direction)
            now = later

    flows = prior_ref[...]
    for i, factor in enumerate(moved):
        flows = flows + factor * basis[i]
    flows_ref[...] = flows
    residual = basis[0]
    for i in range(1, ITERS + 1):
        residual = residual + remaining[i] * basis[i]
    residual_ref[...] = residual


def shards(nets, hours, measured, prior, demand, sigma, coef, tail, head, pipe, count, arrival):
    pipes, length = prior.shape
    cap = pipe.shape[2]
    vmem = pl.BlockSpec(memory_space=pltpu.VMEM)
    smem = pl.BlockSpec(memory_space=pltpu.SMEM)
    field = jax.ShapeDtypeStruct(prior.shape, f32)
    rounds = ITERS + 1
    return pl.pallas_call(
        functools.partial(kernel, nets, hours),
        out_shape=(field, field),
        in_specs=[vmem] * 7 + [smem] * 3,
        out_specs=(vmem, vmem),
        scratch_shapes=[
            pltpu.VMEM((rounds, pipes, length), f32),
            pltpu.VMEM((pipes, length), f32),
            pltpu.VMEM((4, 2, length // 2, length // 2), bf16),
            pltpu.VMEM((rounds, 4 * cap, length), f32),
            pltpu.VMEM((rounds, 6 * cap, length), f32),
            pltpu.VMEM((4 * cap, 128), f32),
            pltpu.VMEM((2, 4 * cap, 128), f32),
            pltpu.VMEM((1, 128), f32),
            pltpu.VMEM((nets * hours - 1, 1, 128), f32),
            pltpu.SemaphoreType.DMA((rounds, 4)),
            pltpu.SemaphoreType.DMA((rounds, 4)),
            pltpu.SemaphoreType.DMA((2,)),
            pltpu.SemaphoreType.DMA((2,)),
            pltpu.SemaphoreType.DMA,
            pltpu.SemaphoreType.DMA,
        ],
        compiler_params=pltpu.CompilerParams(
            collective_id=0, has_side_effects=True, vmem_limit_bytes=32 * 2**20
        ),
        cost_estimate=pl.CostEstimate(
            flops=3 * 8 * 2 * pipes * length * length,
            bytes_accessed=5 * 4 * pipes * length,
            transcendentals=0,
        ),
    )(
        measured,
        prior,
        demand,
        sigma.reshape(1, -1),
        coef.reshape(1, -1),
        tail.reshape(1, -1),
        head.reshape(1, -1),
        pipe,
        count,
        arrival,
    )


def solution(mesh):
    placed = (
        P("net", "hour"),
        P("net", "hour"),
        P("net", "hour"),
        P("net"),
        P(),
        P("net"),
        P("net"),
        P("net", None, None),
        P("net", None),
        P("net", None, None),
    )
    return jax.shard_map(
        functools.partial(shards, mesh.shape["net"], mesh.shape["hour"]),
        mesh=mesh,
        in_specs=placed,
        out_specs=(P("net", "hour"), P("net", "hour")),
        check_vma=False,
    )
```

```python
import functools

import jax
import jax.numpy as jnp
from jax import lax
from jax.experimental import pallas as pl
from jax.experimental.pallas import tpu as pltpu
from jax.sharding import PartitionSpec as P

ITERS = 3
EDGE = 1.5
PENALTY = 4.0
MESH = pl.DeviceIdType.MESH
f32 = jnp.float32
bf16 = jnp.bfloat16


def dot(a, b):
    return jnp.dot(a, b, preferred_element_type=f32)


def split2(x):
    high = x.astype(bf16)
    return high, (x - high.astype(f32)).astype(bf16)


def split3(x):
    high = x.astype(bf16)
    rest = x - high.astype(f32)
    mid = rest.astype(bf16)
    return high, mid, (rest - mid.astype(f32)).astype(bf16)


def total(x):
    return jnp.sum(jnp.sum(x, axis=0, keepdims=True), axis=1, keepdims=True)


def halves(x):
    half = x.shape[1] // 2
    return jnp.concatenate([x[:, :half], x[:, half:]], axis=0)


def joined(x):
    half = x.shape[0] // 2
    return jnp.concatenate([x[:half], x[half:]], axis=1)


def kernel(
    nets,
    hours,
    *refs,
):
    given, refs = refs[:10], refs[10:]
    basis, factors = refs[:2]
    held, refs = refs[2:12], refs[12:]
    (
        measured_ref,
        prior_ref,
        demand_ref,
        sigma_ref,
        coef_ref,
        tail_ref,
        head_ref,
        pipe_ref,
        count_ref,
        arrival_ref,
    ) = held
    (
        load,
        weight,
        toep,
        outgoing,
        incoming,
        pairs_out,
        pairs_in,
        part,
        parts,
        row_send,
        row_recv,
        pair_send,
        pair_recv,
        sum_send,
        sum_recv,
    ) = refs
    loads = [
        pltpu.make_async_copy(src, dst, load.at[i])
        for i, (src, dst) in enumerate(zip(given, held))
    ]
    for i in (9, 8, 7, 6, 5, 1, 2, 4, 3, 0):
        loads[i].start()

    pipes, length = prior_ref.shape
    juncs = demand_ref.shape[0]
    cap = pipe_ref.shape[2]
    half = length // 2
    net = lax.axis_index("net")
    hour = lax.axis_index("hour")
    everyone = nets * hours
    has_left, has_right = net > 0, net < nets - 1
    has_left2, has_right2 = net > 1, net < nets - 2

    def clear(missing, ref):
        @pl.when(missing)
        def _():
            ref[...] = jnp.zeros(ref.shape, f32)

    for r in range(ITERS + 1):
        clear(net == 0, incoming.at[r, pl.ds(0, 2 * cap)])
        clear(net == nets - 1, incoming.at[r, pl.ds(2 * cap, 2 * cap)])
        clear(net < 2, incoming.at[r, pl.ds(4 * cap, cap)])
        clear(net >= nets - 2, incoming.at[r, pl.ds(5 * cap, cap)])
    clear(net == 0, pairs_in.at[0])
    clear(net == nets - 1, pairs_in.at[1])

    barrier = pltpu.get_barrier_semaphore()

    def others():
        for i in range(nets):
            for j in range(hours):
                if i + j > 0:
                    far_net = jnp.where(net + i >= nets, net + i - nets, net + i)
                    far_hour = jnp.where(hour + j >= hours, hour + j - hours, hour + j)
                    yield i * hours + j - 1, (far_net, far_hour)

    for _, peer in others():
        pl.semaphore_signal(barrier, inc=1, device_id=peer, device_id_type=MESH)
    for i in (9, 8, 7, 6, 5):
        loads[i].wait()

    slots = 4 * cap
    sub = lax.broadcasted_iota(jnp.int32, (slots, pipes), 0)
    lane = lax.broadcasted_iota(jnp.int32, (slots, pipes), 1)
    target = jnp.full((slots, pipes), -1, jnp.int32)
    for s in range(2):
        live = count_ref[0, s]
        for k in range(cap):
            own = jnp.where(k < live, pipe_ref[0, s, k], -1)
            target = jnp.where(sub == 2 * s * cap + k, own, target)
    chosen = (lane == target).astype(f32)
    sub_j = lax.broadcasted_iota(jnp.int32, (slots, juncs), 0)
    lane_j = lax.broadcasted_iota(jnp.int32, (slots, juncs), 1)
    landing_at = jnp.full((slots, juncs), -1, jnp.int32)
    for s in range(2):
        for k in range(cap):
            landing_at = jnp.where(
                sub_j == (2 * s + 1) * cap + k, arrival_ref[0, s, k], landing_at
            )
    landing = (lane_j == landing_at).astype(f32)
    interior = 1.0 - jnp.sum(chosen, axis=0, keepdims=True)
    junction = lax.broadcasted_iota(jnp.int32, (juncs, pipes), 0)
    incidence = (junction == head_ref[...]).astype(f32) * interior - (
        junction == tail_ref[...]
    ).astype(f32)
    landing16 = landing.astype(bf16)
    reach = chosen + dot(landing16, incidence.astype(bf16))

    def swapped(x):
        return jnp.concatenate(
            [
                x[cap : 2 * cap],
                x[:cap],
                x[3 * cap :],
                x[2 * cap : 3 * cap],
            ],
            axis=0,
        )

    reach_out = swapped(reach).astype(bf16)
    reach_out3 = jnp.concatenate([reach_out] * 3, axis=1)
    landing_out = swapped(landing).astype(bf16)
    pad_l = jnp.concatenate([landing, jnp.zeros((128 - slots, juncs), f32)], axis=0)
    pairs_out[...] = lax.dot_general(
        landing16,
        pad_l.astype(bf16),
        (((1,), (1,)), ((), ())),
        preferred_element_type=f32,
    )

    loads[4].wait()

    spread = jnp.broadcast_to(coef_ref[...], (half, length))
    rolled = pltpu.roll(spread, 0, 1, stride=1, stride_axis=0)
    at_row = lax.broadcasted_iota(jnp.int32, (half, half), 0)
    at_col = lax.broadcasted_iota(jnp.int32, (half, half), 1)
    near = jnp.where(at_col >= at_row, rolled[:, :half], 0.0)
    far = rolled[:, half:]
    for i, block in enumerate((near, far, near.T, far.T)):
        high, low = split2(block)
        toep[i, 0] = high
        toep[i, 1] = low

    loads[1].wait()
    loads[2].wait()
    prior = prior_ref[...]
    prior_cut = jnp.concatenate(split3(prior), axis=0)
    wanted = jnp.concatenate(split3(demand_ref[...]), axis=0)
    first_out = dot(reach_out3, prior_cut) - dot(
        jnp.concatenate([landing_out] * 3, axis=1), wanted
    )
    outgoing[0] = first_out
    pl.semaphore_wait(barrier, everyone - 1)

    def remote(src, dst, send, recv, shift):
        return pltpu.make_async_remote_copy(
            src_ref=src,
            dst_ref=dst,
            send_sem=send,
            recv_sem=recv,
            device_id=(net + shift, hour),
            device_id_type=MESH,
        )

    def pair_copies():
        yield has_right, has_left, remote(
            pairs_out, pairs_in.at[0], pair_send.at[0], pair_recv.at[0], 1
        )
        yield has_left, has_right, remote(
            pairs_out, pairs_in.at[1], pair_send.at[1], pair_recv.at[1], -1
        )

    def row_copies(r):
        def one(i, start, size, dest, shift):
            return remote(
                outgoing.at[r, pl.ds(start, size)],
                incoming.at[r, pl.ds(dest, size)],
                row_send.at[r, i],
                row_recv.at[r, i],
                shift,
            )

        yield has_right, has_left, one(0, 2 * cap, 2 * cap, 0, 1)
        yield has_left, has_right, one(1, 0, 2 * cap, 2 * cap, -1)
        yield has_right2, has_left2, one(2, 3 * cap, cap, 4 * cap, 2)
        yield has_left2, has_right2, one(3, cap, cap, 5 * cap, -2)

    def start(copies):
        for sends, _, copy in copies:

            @pl.when(sends)
            def _():
                copy.start()

    def arrived(copies):
        for _, receives, copy in copies:

            @pl.when(receives)
            def _():
                copy.wait_recv()

    def left_here(copies):
        for sends, _, copy in copies:

            @pl.when(sends)
            def _():
                copy.wait_send()

    start(pair_copies())
    start(row_copies(0))

    def thrice(high, low, i):
        return (
            dot(high, toep[i, 0]) + dot(low, toep[i, 0]) + dot(high, toep[i, 1])
        )

    def forward(high, low):
        high, low = halves(high), halves(low)
        same = thrice(high, low, 0)
        cross = thrice(high[:pipes], low[:pipes], 1)
        return jnp.concatenate([same[:pipes], same[pipes:] + cross], axis=1)

    def backward(field):
        high, low = split2(halves(field))
        same = thrice(high, low, 2)
        cross = thrice(high[pipes:], low[pipes:], 3)
        return jnp.concatenate([same[:pipes] + cross, same[pipes:]], axis=1)

    loads[3].wait()
    loads[0].wait()
    eye = lax.broadcasted_iota(jnp.int32, (pipes, pipes), 0) == (
        lax.broadcasted_iota(jnp.int32, (pipes, pipes), 1)
    )
    sigma = jnp.sum(jnp.where(eye, sigma_ref[...], 0.0), axis=1, keepdims=True)
    inverse = 1.0 / sigma
    inverse2 = inverse * inverse
    whitened = forward(*split2((measured_ref[...] - prior) * inverse))
    huber = EDGE / jnp.maximum(jnp.abs(whitened), EDGE)
    weight[...] = huber
    near_part = backward(huber * whitened * sigma) * inverse2

    arrived(pair_copies())
    zero = jnp.zeros((cap, pipes), f32)
    fill = jnp.zeros((128 - slots, pipes), f32)
    lower = chosen[:cap]
    upper = chosen[2 * cap : 3 * cap]
    lower_at = jnp.concatenate([zero, zero, zero, lower, fill], axis=0)
    upper_at = jnp.concatenate([zero, upper, zero, zero, fill], axis=0)
    from_left = dot(pairs_in[0].astype(bf16), lower_at.astype(bf16))
    from_right = dot(pairs_in[1].astype(bf16), upper_at.astype(bf16))
    gather = jnp.concatenate(
        [reach, from_left[cap : 2 * cap], from_right[3 * cap :]], axis=0
    )
    width = 6 * cap
    deep = -(-3 * width // 128) * 128
    gather3 = jnp.concatenate(
        [gather] * 3 + [jnp.zeros((deep - 3 * width, pipes), f32)], axis=0
    )
    spread_in = (PENALTY * gather3.T).astype(bf16)
    tall = -(-(juncs + 2 * cap) // 128) * 128
    rest = jnp.zeros((tall - juncs - 2 * cap, pipes), f32)
    left_side = jnp.concatenate([incidence, lower, upper, rest], axis=0).T
    right_side = jnp.concatenate(
        [incidence, from_left[3 * cap :], from_right[cap : 2 * cap], rest], axis=0
    )
    local = (
        PENALTY * dot(left_side.astype(bf16), right_side.astype(bf16))
    ).astype(bf16)
    local3 = jnp.concatenate([local] * 3, axis=1)
    back = (PENALTY * left_side).astype(bf16)
    empty = jnp.zeros((tall - juncs, length), bf16)
    wanted = jnp.concatenate(
        [
            x
            for i in range(3)
            for x in (wanted[i * juncs : (i + 1) * juncs], empty)
        ],
        axis=0,
    )
    tail_rows = jnp.zeros((deep - 3 * width, length), bf16)

    def received(r):
        arrived(row_copies(r))
        cut = jnp.concatenate(split3(incoming[r]) + (tail_rows,), axis=0)
        return dot(spread_in, cut)

    here = near_part + dot(jnp.concatenate([back] * 3, axis=1), wanted)
    here = here - dot(local3, prior_cut)
    vector = here - received(0)

    def operator(r, field, beside=None):
        pieces = split3(field)
        cut = jnp.concatenate(pieces, axis=0)
        outgoing[r] = dot(reach_out3, cut)
        start(row_copies(r))
        if beside is not None:
            beside()
        here = dot(local3, cut)
        filtered = forward(pieces[0], pieces[1])
        here = here + backward(weight[...] * filtered) * inverse2
        return here + received(r)

    at = lax.broadcasted_iota(jnp.int32, (1, 128), 1)

    def share(i, values):
        mine = jnp.zeros((1, 128), f32)
        for k, value in enumerate(values):
            mine = jnp.where(at == k, value, mine)
        part[i] = mine
        for slot, peer in others():
            pltpu.make_async_remote_copy(
                src_ref=part.at[i],
                dst_ref=parts.at[i, slot],
                send_sem=sum_send.at[i],
                recv_sem=sum_recv.at[i],
                device_id=peer,
                device_id_type=MESH,
            ).start()

    def shared(i, count):
        pltpu.make_async_copy(parts.at[i], parts.at[i], sum_recv.at[i]).wait()
        sums = part[i] + jnp.sum(parts[i], axis=0)
        return [sums[:, k : k + 1] for k in range(count)]

    start0 = vector
    basis[0] = start0
    square = total(start0 * start0)
    image0 = operator(1, start0)
    image00 = operator(2, image0, lambda: share(0, [square, total(start0 * image0)]))
    square, curve = shared(0, 2)
    first = square / curve
    after = start0 - first * image0
    image = first * (image0 - first * image00)
    basis[1] = after
    basis[2] = image
    known = []

    def hidden():
        pairs = ((start0, after), (start0, image), (after, after), (after, image), (image, image))
        known.extend(total(x * y) for x, y in pairs)

    image2 = first * operator(3, image, hidden)
    basis[3] = image2
    share(1, known + [total(x * image2) for x in (start0, after, image)])
    for r in range(ITERS + 1):
        left_here(row_copies(r))
    left_here(pair_copies())
    pltpu.make_async_copy(parts.at[0], parts.at[0], sum_send.at[0]).wait()
    sa, si, aa, ai, ii, sj, aj, ij = shared(1, 8)
    pltpu.make_async_copy(parts.at[1], parts.at[1], sum_send.at[1]).wait()
    gram = ((square, sa, si, sj), (sa, aa, ai, aj), (si, ai, ii, ij))

    def product(a, b):
        out = None
        for i in range(4):
            for j in range(4):
                if i < 3 or j < 3:
                    term = a[i] * b[j] * (gram[i][j] if i < 3 else gram[j][i])
                    out = term if out is None else out + term
        return out

    zero = jnp.zeros((1, 1), f32)
    one = jnp.ones((1, 1), f32)
    remaining = [zero, one, zero, zero]
    now = aa
    direction = [now / square, one, zero, zero]
    moved = [one, zero, zero, zero]
    for i in range(1, ITERS):
        applied = [direction[0], -direction[0], direction[1], direction[2]]
        step = now / product(direction, applied)
        moved = [x + step * y for x, y in zip(moved, direction)]
        remaining = [x - step * y for x, y in zip(remaining, applied)]
        if i + 1 < ITERS:
            later = product(remaining, remaining)
            direction = [x + later / now * y for x, y in zip(remaining, direction)]
            now = later
    for i, factor in enumerate([first * x for x in moved[:3]] + remaining):
        factors[i] = jnp.broadcast_to(factor, (1, length))


def combine(prior_ref, basis_ref, factors_ref, flows_ref, residual_ref):
    flows, residual = prior_ref[...], factors_ref[3] * basis_ref[0]
    for i in range(3):
        flows = flows + factors_ref[i] * basis_ref[i]
        residual = residual + factors_ref[4 + i] * basis_ref[1 + i]
    flows_ref[...] = flows
    residual_ref[...] = residual


def shards(nets, hours, *args):
    prior, demand, pipe = args[1], args[2], args[7]
    pipes, length = prior.shape
    cap = pipe.shape[2]
    args = [x.reshape(1, -1) if x.ndim == 1 else x for x in args]
    args = [pltpu.with_memory_space_constraint(x, pltpu.HBM) for x in args]
    vmem = pl.BlockSpec(memory_space=pltpu.VMEM)
    rounds = ITERS + 1
    basis, factors = pl.pallas_call(
        functools.partial(kernel, nets, hours),
        out_shape=(
            jax.ShapeDtypeStruct((rounds, pipes, length), f32),
            jax.ShapeDtypeStruct((7, 1, length), f32),
        ),
        in_specs=[pl.BlockSpec(memory_space=pltpu.HBM)] * 10,
        out_specs=(vmem, vmem),
        scratch_shapes=[pltpu.VMEM(x.shape, x.dtype) for x in args[:7]]
        + [pltpu.SMEM(x.shape, x.dtype) for x in args[7:]]
        + [
            pltpu.SemaphoreType.DMA((10,)),
            pltpu.VMEM((pipes, length), f32),
            pltpu.VMEM((4, 2, length // 2, length // 2), bf16),
            pltpu.VMEM((rounds, 4 * cap, length), f32),
            pltpu.VMEM((rounds, 6 * cap, length), f32),
            pltpu.VMEM((4 * cap, 128), f32),
            pltpu.VMEM((2, 4 * cap, 128), f32),
            pltpu.VMEM((2, 1, 128), f32),
            pltpu.VMEM((2, nets * hours - 1, 1, 128), f32),
            pltpu.SemaphoreType.DMA((rounds, 4)),
            pltpu.SemaphoreType.DMA((rounds, 4)),
            pltpu.SemaphoreType.DMA((2,)),
            pltpu.SemaphoreType.DMA((2,)),
            pltpu.SemaphoreType.DMA((2,)),
            pltpu.SemaphoreType.DMA((2,)),
        ],
        compiler_params=pltpu.CompilerParams(
            collective_id=0, has_side_effects=True, vmem_limit_bytes=32 * 2**20
        ),
        cost_estimate=pl.CostEstimate(
            flops=3 * 8 * 2 * pipes * length * length,
            bytes_accessed=5 * 4 * pipes * length,
            transcendentals=0,
        ),
    )(*args)
    field = jax.ShapeDtypeStruct(prior.shape, f32)
    return pl.pallas_call(
        combine,
        out_shape=(field, field),
        in_specs=[vmem] * 3,
        out_specs=(vmem, vmem),
    )(prior, basis, factors)


def solution(mesh):
    placed = (
        P("net", "hour"),
        P("net", "hour"),
        P("net", "hour"),
        P("net"),
        P(),
        P("net"),
        P("net"),
        P("net", None, None),
        P("net", None),
        P("net", None, None),
    )
    return jax.shard_map(
        functools.partial(shards, mesh.shape["net"], mesh.shape["hour"]),
        mesh=mesh,
        in_specs=placed,
        out_specs=(P("net", "hour"), P("net", "hour")),
        check_vma=False,
    )
```

```python
import functools

import jax
import jax.numpy as jnp
from jax import lax
from jax.experimental import pallas as pl
from jax.experimental.pallas import tpu as pltpu
from jax.sharding import PartitionSpec as P

ITERS = 3
EDGE = 1.5
PENALTY = 4.0
MESH = pl.DeviceIdType.MESH
f32 = jnp.float32
bf16 = jnp.bfloat16


def dot(a, b):
    return jnp.dot(a, b, preferred_element_type=f32)


def split2(x):
    high = x.astype(bf16)
    return high, (x - high.astype(f32)).astype(bf16)


def cut2(x):
    return jnp.concatenate(split2(x), axis=0)


def total(x):
    return jnp.sum(jnp.sum(x, axis=0, keepdims=True), axis=1, keepdims=True)


def halves(x):
    half = x.shape[1] // 2
    return jnp.concatenate([x[:, :half], x[:, half:]], axis=0)


def joined(x):
    half = x.shape[0] // 2
    return jnp.concatenate([x[:half], x[half:]], axis=1)


def kernel(
    nets,
    hours,
    *refs,
):
    given, refs = refs[:10], refs[10:]
    flows_ref, residual_ref = refs[:2]
    held, refs = refs[2:12], refs[12:]
    (
        measured_ref,
        prior_ref,
        demand_ref,
        sigma_ref,
        coef_ref,
        tail_ref,
        head_ref,
        pipe_ref,
        count_ref,
        arrival_ref,
    ) = held
    (
        load,
        weight,
        toep,
        outgoing,
        incoming,
        pairs_out,
        pairs_in,
        basis,
        part_hour,
        part_net,
        parts_hour,
        parts_net,
        row_send,
        row_recv,
        pair_send,
        pair_recv,
        hour_send,
        hour_recv,
        net_send,
        net_recv,
    ) = refs
    loads = [
        pltpu.make_async_copy(src, dst, load.at[i])
        for i, (src, dst) in enumerate(zip(given, held))
    ]
    for i in (9, 8, 7, 6, 5, 1, 2, 4, 3, 0):
        loads[i].start()

    pipes, length = prior_ref.shape
    juncs = demand_ref.shape[0]
    cap = pipe_ref.shape[2]
    half = length // 2
    net = lax.axis_index("net")
    hour = lax.axis_index("hour")
    has_left, has_right = net > 0, net < nets - 1
    has_left2, has_right2 = net > 1, net < nets - 2

    def clear(missing, ref):
        @pl.when(missing)
        def _():
            ref[...] = jnp.zeros(ref.shape, f32)

    for r in range(ITERS + 1):
        clear(net == 0, incoming.at[r, pl.ds(0, 2 * cap)])
        clear(net == nets - 1, incoming.at[r, pl.ds(2 * cap, 2 * cap)])
        clear(net < 2, incoming.at[r, pl.ds(4 * cap, cap)])
        clear(net >= nets - 2, incoming.at[r, pl.ds(5 * cap, cap)])
    clear(net == 0, pairs_in.at[0])
    clear(net == nets - 1, pairs_in.at[1])

    barrier = pltpu.get_barrier_semaphore()

    def ring(at, count):
        for i in range(1, count):
            yield i - 1, jnp.where(at + i >= count, at + i - count, at + i)

    hour_peers = [(slot, (net, far)) for slot, far in ring(hour, hours)]
    net_peers = [(slot, (far, hour)) for slot, far in ring(net, nets)]
    for _, peer in hour_peers + net_peers:
        pl.semaphore_signal(barrier, inc=1, device_id=peer, device_id_type=MESH)
    for i in (9, 8, 7, 6, 5):
        loads[i].wait()

    slots = 4 * cap
    sub = lax.broadcasted_iota(jnp.int32, (slots, pipes), 0)
    lane = lax.broadcasted_iota(jnp.int32, (slots, pipes), 1)
    target = jnp.full((slots, pipes), -1, jnp.int32)
    for s in range(2):
        live = count_ref[0, s]
        for k in range(cap):
            own = jnp.where(k < live, pipe_ref[0, s, k], -1)
            target = jnp.where(sub == 2 * s * cap + k, own, target)
    chosen = (lane == target).astype(f32)
    sub_j = lax.broadcasted_iota(jnp.int32, (slots, juncs), 0)
    lane_j = lax.broadcasted_iota(jnp.int32, (slots, juncs), 1)
    landing_at = jnp.full((slots, juncs), -1, jnp.int32)
    for s in range(2):
        for k in range(cap):
            landing_at = jnp.where(
                sub_j == (2 * s + 1) * cap + k, arrival_ref[0, s, k], landing_at
            )
    landing = (lane_j == landing_at).astype(f32)
    interior = 1.0 - jnp.sum(chosen, axis=0, keepdims=True)
    junction = lax.broadcasted_iota(jnp.int32, (juncs, pipes), 0)
    incidence = (junction == head_ref[...]).astype(f32) * interior - (
        junction == tail_ref[...]
    ).astype(f32)
    landing16 = landing.astype(bf16)
    reach = chosen + dot(landing16, incidence.astype(bf16))

    def swapped(x):
        return jnp.concatenate(
            [
                x[cap : 2 * cap],
                x[:cap],
                x[3 * cap :],
                x[2 * cap : 3 * cap],
            ],
            axis=0,
        )

    reach_out = swapped(reach).astype(bf16)
    reach_out2 = jnp.concatenate([reach_out] * 2, axis=1)
    landing_out = swapped(landing).astype(bf16)
    pad_l = jnp.concatenate([landing, jnp.zeros((128 - slots, juncs), f32)], axis=0)
    pairs_out[...] = lax.dot_general(
        landing16,
        pad_l.astype(bf16),
        (((1,), (1,)), ((), ())),
        preferred_element_type=f32,
    )

    loads[1].wait()
    loads[2].wait()
    prior = prior_ref[...]
    prior_cut = cut2(prior)
    wanted = cut2(demand_ref[...])
    outgoing[0] = dot(reach_out2, prior_cut) - dot(
        jnp.concatenate([landing_out] * 2, axis=1), wanted
    )
    pl.semaphore_wait(barrier, len(hour_peers) + len(net_peers))

    def remote(src, dst, send, recv, shift):
        return pltpu.make_async_remote_copy(
            src_ref=src,
            dst_ref=dst,
            send_sem=send,
            recv_sem=recv,
            device_id=(net + shift, hour),
            device_id_type=MESH,
        )

    def pair_copies():
        yield has_right, has_left, remote(
            pairs_out, pairs_in.at[0], pair_send.at[0], pair_recv.at[0], 1
        )
        yield has_left, has_right, remote(
            pairs_out, pairs_in.at[1], pair_send.at[1], pair_recv.at[1], -1
        )

    def row_copies(r):
        def one(i, start, size, dest, shift):
            return remote(
                outgoing.at[r, pl.ds(start, size)],
                incoming.at[r, pl.ds(dest, size)],
                row_send.at[r, i],
                row_recv.at[r, i],
                shift,
            )

        yield has_right, has_left, one(0, 2 * cap, 2 * cap, 0, 1)
        yield has_left, has_right, one(1, 0, 2 * cap, 2 * cap, -1)
        yield has_right2, has_left2, one(2, 3 * cap, cap, 4 * cap, 2)
        yield has_left2, has_right2, one(3, cap, cap, 5 * cap, -2)

    def start(copies):
        for sends, _, copy in copies:

            @pl.when(sends)
            def _():
                copy.start()

    def arrived(copies):
        for _, receives, copy in copies:

            @pl.when(receives)
            def _():
                copy.wait_recv()

    def left_here(copies):
        for sends, _, copy in copies:

            @pl.when(sends)
            def _():
                copy.wait_send()

    start(pair_copies())
    start(row_copies(0))
    loads[4].wait()

    spread = jnp.broadcast_to(coef_ref[...], (half, length))
    rolled = pltpu.roll(spread, 0, 1, stride=1, stride_axis=0)
    at_row = lax.broadcasted_iota(jnp.int32, (half, half), 0)
    at_col = lax.broadcasted_iota(jnp.int32, (half, half), 1)
    near = jnp.where(at_col >= at_row, rolled[:, :half], 0.0)
    far = rolled[:, half:]
    for i, block in enumerate((near, far, near.T, far.T)):
        high, low = split2(block)
        toep[i, 0] = high
        toep[i, 1] = low


    def thrice(high, low, i):
        return (
            dot(high, toep[i, 0]) + dot(low, toep[i, 0]) + dot(high, toep[i, 1])
        )

    def forward(high, low):
        high, low = halves(high), halves(low)
        same = thrice(high, low, 0)
        cross = thrice(high[:pipes], low[:pipes], 1)
        return jnp.concatenate([same[:pipes], same[pipes:] + cross], axis=1)

    def backward(field):
        high, low = split2(halves(field))
        same = thrice(high, low, 2)
        cross = thrice(high[pipes:], low[pipes:], 3)
        return jnp.concatenate([same[:pipes] + cross, same[pipes:]], axis=1)

    loads[3].wait()
    loads[0].wait()
    eye = lax.broadcasted_iota(jnp.int32, (pipes, pipes), 0) == (
        lax.broadcasted_iota(jnp.int32, (pipes, pipes), 1)
    )
    sigma = jnp.sum(jnp.where(eye, sigma_ref[...], 0.0), axis=1, keepdims=True)
    inverse = 1.0 / sigma
    inverse2 = inverse * inverse
    whitened = forward(*split2((measured_ref[...] - prior) * inverse))
    huber = EDGE / jnp.maximum(jnp.abs(whitened), EDGE)
    weight[...] = huber
    near_part = backward(huber * whitened * sigma) * inverse2

    arrived(pair_copies())
    zero = jnp.zeros((cap, pipes), f32)
    fill = jnp.zeros((128 - slots, pipes), f32)
    lower = chosen[:cap]
    upper = chosen[2 * cap : 3 * cap]
    lower_at = jnp.concatenate([zero, zero, zero, lower, fill], axis=0)
    upper_at = jnp.concatenate([zero, upper, zero, zero, fill], axis=0)
    from_left = dot(pairs_in[0].astype(bf16), lower_at.astype(bf16))
    from_right = dot(pairs_in[1].astype(bf16), upper_at.astype(bf16))
    gather = jnp.concatenate(
        [reach, from_left[cap : 2 * cap], from_right[3 * cap :]], axis=0
    )
    width = 6 * cap
    deep = -(-2 * width // 128) * 128
    gather2 = jnp.concatenate(
        [gather] * 2 + [jnp.zeros((deep - 2 * width, pipes), f32)], axis=0
    )
    spread_in = (PENALTY * gather2.T).astype(bf16)
    onward = dot(reach_out, spread_in).astype(bf16)
    tall = -(-(juncs + 2 * cap) // 128) * 128
    rest = jnp.zeros((tall - juncs - 2 * cap, pipes), f32)
    left_side = jnp.concatenate([incidence, lower, upper, rest], axis=0).T
    right_side = jnp.concatenate(
        [incidence, from_left[3 * cap :], from_right[cap : 2 * cap], rest], axis=0
    )
    local = (
        PENALTY * dot(left_side.astype(bf16), right_side.astype(bf16))
    ).astype(bf16)
    local2 = jnp.concatenate([local] * 2, axis=1)
    back = (PENALTY * left_side).astype(bf16)
    empty = jnp.zeros((tall - juncs, length), bf16)
    wanted = jnp.concatenate([wanted[:juncs], empty, wanted[juncs:], empty], axis=0)
    tail_rows = jnp.zeros((deep - 2 * width, length), bf16)

    def received(r):
        arrived(row_copies(r))
        return jnp.concatenate(split2(incoming[r]) + (tail_rows,), axis=0)

    def send(r, rows):
        outgoing[r] = rows
        start(row_copies(r))

    def near(field, beside=None):
        pieces = split2(field)
        here = dot(local2, jnp.concatenate(pieces, axis=0))
        filtered = forward(*pieces)
        if beside is not None:
            beside()
        return here + backward(weight[...] * filtered) * inverse2

    def rows_of(field):
        return dot(reach_out2, cut2(field))

    at = lax.broadcasted_iota(jnp.int32, (1, 128), 1)

    def post(mine, theirs, peers, sent, came, i):
        for slot, peer in peers:
            pltpu.make_async_remote_copy(
                src_ref=mine.at[i],
                dst_ref=theirs.at[i, slot],
                send_sem=sent.at[i],
                recv_sem=came.at[i],
                device_id=peer,
                device_id_type=MESH,
            ).start()

    def whole(theirs, sem, i):
        pltpu.make_async_copy(theirs.at[i], theirs.at[i], sem.at[i]).wait()

    def share_hours(i, values):
        mine = jnp.zeros((1, 128), f32)
        for k, value in enumerate(values):
            mine = jnp.where(at == k, value, mine)
        part_hour[i] = mine
        post(part_hour, parts_hour, hour_peers, hour_send, hour_recv, i)

    def share_nets(i):
        whole(parts_hour, hour_recv, i)
        part_net[i] = part_hour[i] + jnp.sum(parts_hour[i], axis=0)
        post(part_net, parts_net, net_peers, net_send, net_recv, i)

    def shared(i, count):
        whole(parts_net, net_recv, i)
        sums = part_net[i] + jnp.sum(parts_net[i], axis=0)
        return [sums[:, k : k + 1] for k in range(count)]

    here = near_part + dot(jnp.concatenate([back] * 2, axis=1), wanted)
    here = here - dot(local2, prior_cut)
    rows = rows_of(here)
    came = received(0)
    send(1, rows - dot(onward, came))
    start0 = here - dot(spread_in, came)
    basis[0] = start0
    square = total(start0 * start0)
    here = near(start0)
    rows = rows_of(here)
    came = received(1)
    send(2, rows + dot(onward, came))
    image0 = here + dot(spread_in, came)
    share_hours(0, [square, total(start0 * image0)])
    here = near(image0, lambda: share_nets(0))
    rows = rows_of(here)
    came = received(2)
    rows = rows + dot(onward, came)
    square, curve = shared(0, 2)
    first = square / curve
    send(3, first * (outgoing[2] - first * rows))
    image00 = here + dot(spread_in, came)
    start0 = basis[0]
    after = start0 - first * image0
    image = first * (image0 - first * image00)
    basis[1] = after
    basis[2] = image
    pairs = ((start0, after), (start0, image), (after, after), (after, image), (image, image))
    known = [total(x * y) for x, y in pairs]
    here = near(image)
    came = received(3)
    image2 = first * (here + dot(spread_in, came))
    basis[3] = image2
    share_hours(1, known + [total(x * image2) for x in (basis[0], basis[1], basis[2])])
    for r in range(ITERS + 1):
        left_here(row_copies(r))
    left_here(pair_copies())
    whole(parts_hour, hour_send, 0)
    whole(parts_net, net_send, 0)
    share_nets(1)
    whole(parts_hour, hour_send, 1)
    sa, si, aa, ai, ii, sj, aj, ij = shared(1, 8)
    whole(parts_net, net_send, 1)
    gram = ((square, sa, si, sj), (sa, aa, ai, aj), (si, ai, ii, ij))

    def product(a, b):
        out = None
        for i in range(4):
            for j in range(4):
                if i < 3 or j < 3:
                    term = a[i] * b[j] * (gram[i][j] if i < 3 else gram[j][i])
                    out = term if out is None else out + term
        return out

    zero = jnp.zeros((1, 1), f32)
    one = jnp.ones((1, 1), f32)
    remaining = [zero, one, zero, zero]
    now = aa
    direction = [now / square, one, zero, zero]
    moved = [one, zero, zero, zero]
    for i in range(1, ITERS):
        applied = [direction[0], -direction[0], direction[1], direction[2]]
        step = now / product(direction, applied)
        moved = [x + step * y for x, y in zip(moved, direction)]
        remaining = [x - step * y for x, y in zip(remaining, applied)]
        if i + 1 < ITERS:
            later = product(remaining, remaining)
            direction = [x + later / now * y for x, y in zip(remaining, direction)]
            now = later
    flows, residual = prior_ref[...], remaining[3] * basis[3]
    for i in range(3):
        flows = flows + first * moved[i] * basis[i]
        residual = residual + remaining[i] * basis[i]
    flows_ref[...] = flows
    residual_ref[...] = residual


def shards(nets, hours, *args):
    prior, demand, pipe = args[1], args[2], args[7]
    pipes, length = prior.shape
    cap = pipe.shape[2]
    args = [x.reshape(1, -1) if x.ndim == 1 else x for x in args]
    args = [pltpu.with_memory_space_constraint(x, pltpu.HBM) for x in args]
    vmem = pl.BlockSpec(memory_space=pltpu.VMEM)
    rounds = ITERS + 1
    field = jax.ShapeDtypeStruct(prior.shape, f32)
    return pl.pallas_call(
        functools.partial(kernel, nets, hours),
        out_shape=(field, field),
        in_specs=[pl.BlockSpec(memory_space=pltpu.HBM)] * 10,
        out_specs=(vmem, vmem),
        scratch_shapes=[pltpu.VMEM(x.shape, x.dtype) for x in args[:7]]
        + [pltpu.SMEM(x.shape, x.dtype) for x in args[7:]]
        + [
            pltpu.SemaphoreType.DMA((10,)),
            pltpu.VMEM((pipes, length), f32),
            pltpu.VMEM((4, 2, length // 2, length // 2), bf16),
            pltpu.VMEM((rounds, 4 * cap, length), f32),
            pltpu.VMEM((rounds, 6 * cap, length), f32),
            pltpu.VMEM((4 * cap, 128), f32),
            pltpu.VMEM((2, 4 * cap, 128), f32),
            pltpu.VMEM((rounds, pipes, length), f32),
            pltpu.VMEM((2, 1, 128), f32),
            pltpu.VMEM((2, 1, 128), f32),
            pltpu.VMEM((2, hours - 1, 1, 128), f32),
            pltpu.VMEM((2, nets - 1, 1, 128), f32),
            pltpu.SemaphoreType.DMA((rounds, 4)),
            pltpu.SemaphoreType.DMA((rounds, 4)),
            pltpu.SemaphoreType.DMA((2,)),
            pltpu.SemaphoreType.DMA((2,)),
            pltpu.SemaphoreType.DMA((2,)),
            pltpu.SemaphoreType.DMA((2,)),
            pltpu.SemaphoreType.DMA((2,)),
            pltpu.SemaphoreType.DMA((2,)),
        ],
        compiler_params=pltpu.CompilerParams(
            collective_id=0, has_side_effects=True, vmem_limit_bytes=32 * 2**20
        ),
        cost_estimate=pl.CostEstimate(
            flops=3 * 8 * 2 * pipes * length * length,
            bytes_accessed=5 * 4 * pipes * length,
            transcendentals=0,
        ),
    )(*args)

def solution(mesh):
    placed = (
        P("net", "hour"),
        P("net", "hour"),
        P("net", "hour"),
        P("net"),
        P(),
        P("net"),
        P("net"),
        P("net", None, None),
        P("net", None),
        P("net", None, None),
    )
    return jax.shard_map(
        functools.partial(shards, mesh.shape["net"], mesh.shape["hour"]),
        mesh=mesh,
        in_specs=placed,
        out_specs=(P("net", "hour"), P("net", "hour")),
        check_vma=False,
    )
```

```python
import functools

import jax
import jax.numpy as jnp
from jax import lax
from jax.experimental import pallas as pl
from jax.experimental.pallas import tpu as pltpu
from jax.sharding import PartitionSpec as P

ITERS = 3
EDGE = 1.5
PENALTY = 4.0
MESH = pl.DeviceIdType.MESH
f32 = jnp.float32
bf16 = jnp.bfloat16


def dot(a, b):
    return jnp.dot(a, b, preferred_element_type=f32)


def split2(x):
    high = x.astype(bf16)
    return high, (x - high.astype(f32)).astype(bf16)


def cut2(x):
    return jnp.concatenate(split2(x), axis=0)


def total(x):
    return jnp.sum(jnp.sum(x, axis=0, keepdims=True), axis=1, keepdims=True)


def halves(x):
    half = x.shape[1] // 2
    return jnp.concatenate([x[:, :half], x[:, half:]], axis=0)


def joined(x):
    half = x.shape[0] // 2
    return jnp.concatenate([x[:half], x[half:]], axis=1)


def kernel(
    nets,
    hours,
    *refs,
):
    given, refs = refs[:10], refs[10:]
    flows_ref, residual_ref = refs[:2]
    held, refs = refs[2:12], refs[12:]
    (
        measured_ref,
        prior_ref,
        demand_ref,
        sigma_ref,
        coef_ref,
        tail_ref,
        head_ref,
        pipe_ref,
        count_ref,
        arrival_ref,
    ) = held
    (
        load,
        weight,
        toep,
        outgoing,
        incoming,
        pairs_out,
        pairs_in,
        basis,
        part,
        parts,
        row_send,
        row_recv,
        pair_send,
        pair_recv,
        sum_send,
        sum_recv,
    ) = refs
    loads = [
        pltpu.make_async_copy(src, dst, load.at[i])
        for i, (src, dst) in enumerate(zip(given, held))
    ]
    for i in (9, 8, 7, 6, 5, 1, 2, 4, 3, 0):
        loads[i].start()

    pipes, length = prior_ref.shape
    juncs = demand_ref.shape[0]
    cap = pipe_ref.shape[2]
    half = length // 2
    net = lax.axis_index("net")
    hour = lax.axis_index("hour")
    has_left, has_right = net > 0, net < nets - 1
    has_left2, has_right2 = net > 1, net < nets - 2

    def clear(missing, ref):
        @pl.when(missing)
        def _():
            ref[...] = jnp.zeros(ref.shape, f32)

    for r in range(ITERS + 1):
        clear(net == 0, incoming.at[r, pl.ds(0, 2 * cap)])
        clear(net == nets - 1, incoming.at[r, pl.ds(2 * cap, 2 * cap)])
        clear(net < 2, incoming.at[r, pl.ds(4 * cap, cap)])
        clear(net >= nets - 2, incoming.at[r, pl.ds(5 * cap, cap)])
    clear(net == 0, pairs_in.at[0])
    clear(net == nets - 1, pairs_in.at[1])

    barrier = pltpu.get_barrier_semaphore()

    def others():
        for i in range(nets):
            for j in range(hours):
                if i + j > 0:
                    far_net = jnp.where(net + i >= nets, net + i - nets, net + i)
                    far_hour = jnp.where(hour + j >= hours, hour + j - hours, hour + j)
                    yield i * hours + j - 1, (far_net, far_hour)

    for _, peer in others():
        pl.semaphore_signal(barrier, inc=1, device_id=peer, device_id_type=MESH)
    for i in (9, 8, 7, 6, 5):
        loads[i].wait()

    slots = 4 * cap
    sub = lax.broadcasted_iota(jnp.int32, (slots, pipes), 0)
    lane = lax.broadcasted_iota(jnp.int32, (slots, pipes), 1)
    target = jnp.full((slots, pipes), -1, jnp.int32)
    for s in range(2):
        live = count_ref[0, s]
        for k in range(cap):
            own = jnp.where(k < live, pipe_ref[0, s, k], -1)
            target = jnp.where(sub == 2 * s * cap + k, own, target)
    chosen = (lane == target).astype(f32)
    sub_j = lax.broadcasted_iota(jnp.int32, (slots, juncs), 0)
    lane_j = lax.broadcasted_iota(jnp.int32, (slots, juncs), 1)
    landing_at = jnp.full((slots, juncs), -1, jnp.int32)
    for s in range(2):
        for k in range(cap):
            landing_at = jnp.where(
                sub_j == (2 * s + 1) * cap + k, arrival_ref[0, s, k], landing_at
            )
    landing = (lane_j == landing_at).astype(f32)
    interior = 1.0 - jnp.sum(chosen, axis=0, keepdims=True)
    junction = lax.broadcasted_iota(jnp.int32, (juncs, pipes), 0)
    incidence = (junction == head_ref[...]).astype(f32) * interior - (
        junction == tail_ref[...]
    ).astype(f32)
    landing16 = landing.astype(bf16)
    reach = chosen + dot(landing16, incidence.astype(bf16))

    def swapped(x):
        return jnp.concatenate(
            [
                x[cap : 2 * cap],
                x[:cap],
                x[3 * cap :],
                x[2 * cap : 3 * cap],
            ],
            axis=0,
        )

    reach_out = swapped(reach).astype(bf16)
    reach_out2 = jnp.concatenate([reach_out] * 2, axis=1)
    landing_out = swapped(landing).astype(bf16)
    pad_l = jnp.concatenate([landing, jnp.zeros((128 - slots, juncs), f32)], axis=0)
    pairs_out[...] = lax.dot_general(
        landing16,
        pad_l.astype(bf16),
        (((1,), (1,)), ((), ())),
        preferred_element_type=f32,
    )

    loads[1].wait()
    loads[2].wait()
    prior = prior_ref[...]
    prior_cut = cut2(prior)
    wanted = cut2(demand_ref[...])
    outgoing[0] = dot(reach_out2, prior_cut) - dot(
        jnp.concatenate([landing_out] * 2, axis=1), wanted
    )
    pl.semaphore_wait(barrier, nets * hours - 1)

    def remote(src, dst, send, recv, shift):
        return pltpu.make_async_remote_copy(
            src_ref=src,
            dst_ref=dst,
            send_sem=send,
            recv_sem=recv,
            device_id=(net + shift, hour),
            device_id_type=MESH,
        )

    def pair_copies():
        yield has_right, has_left, remote(
            pairs_out, pairs_in.at[0], pair_send.at[0], pair_recv.at[0], 1
        )
        yield has_left, has_right, remote(
            pairs_out, pairs_in.at[1], pair_send.at[1], pair_recv.at[1], -1
        )

    def row_copies(r):
        def one(i, start, size, dest, shift):
            return remote(
                outgoing.at[r, pl.ds(start, size)],
                incoming.at[r, pl.ds(dest, size)],
                row_send.at[r, i],
                row_recv.at[r, i],
                shift,
            )

        yield has_right, has_left, one(0, 2 * cap, 2 * cap, 0, 1)
        yield has_left, has_right, one(1, 0, 2 * cap, 2 * cap, -1)
        yield has_right2, has_left2, one(2, 3 * cap, cap, 4 * cap, 2)
        yield has_left2, has_right2, one(3, cap, cap, 5 * cap, -2)

    def start(copies):
        for sends, _, copy in copies:

            @pl.when(sends)
            def _():
                copy.start()

    def arrived(copies):
        for _, receives, copy in copies:

            @pl.when(receives)
            def _():
                copy.wait_recv()

    def left_here(copies):
        for sends, _, copy in copies:

            @pl.when(sends)
            def _():
                copy.wait_send()

    start(pair_copies())
    start(row_copies(0))
    loads[4].wait()

    spread = jnp.broadcast_to(coef_ref[...], (half, length))
    rolled = pltpu.roll(spread, 0, 1, stride=1, stride_axis=0)
    at_row = lax.broadcasted_iota(jnp.int32, (half, half), 0)
    at_col = lax.broadcasted_iota(jnp.int32, (half, half), 1)
    near = jnp.where(at_col >= at_row, rolled[:, :half], 0.0)
    far = rolled[:, half:]
    for i, block in enumerate((near, far, near.T, far.T)):
        high, low = split2(block)
        toep[i, pl.ds(0, half)] = high
        toep[i, pl.ds(half, half)] = high
        toep[i, pl.ds(2 * half, half)] = low


    def thrice(high, low, i):
        return dot(jnp.concatenate([high, low, high], axis=1), toep[i])

    def forward(high, low):
        high, low = halves(high), halves(low)
        same = thrice(high, low, 0)
        cross = thrice(high[:pipes], low[:pipes], 1)
        return jnp.concatenate([same[:pipes], same[pipes:] + cross], axis=1)

    def backward(field):
        high, low = split2(halves(field))
        same = thrice(high, low, 2)
        cross = thrice(high[pipes:], low[pipes:], 3)
        return jnp.concatenate([same[:pipes] + cross, same[pipes:]], axis=1)

    loads[3].wait()
    loads[0].wait()
    eye = lax.broadcasted_iota(jnp.int32, (pipes, pipes), 0) == (
        lax.broadcasted_iota(jnp.int32, (pipes, pipes), 1)
    )
    sigma = jnp.sum(jnp.where(eye, sigma_ref[...], 0.0), axis=1, keepdims=True)
    inverse = 1.0 / sigma
    inverse2 = inverse * inverse
    whitened = forward(*split2((measured_ref[...] - prior) * inverse))
    huber = EDGE / jnp.maximum(jnp.abs(whitened), EDGE)
    weight[...] = huber
    near_part = backward(huber * whitened * sigma) * inverse2

    arrived(pair_copies())
    zero = jnp.zeros((cap, pipes), f32)
    fill = jnp.zeros((128 - slots, pipes), f32)
    lower = chosen[:cap]
    upper = chosen[2 * cap : 3 * cap]
    lower_at = jnp.concatenate([zero, zero, zero, lower, fill], axis=0)
    upper_at = jnp.concatenate([zero, upper, zero, zero, fill], axis=0)
    from_left = dot(pairs_in[0].astype(bf16), lower_at.astype(bf16))
    from_right = dot(pairs_in[1].astype(bf16), upper_at.astype(bf16))
    gather = jnp.concatenate(
        [reach, from_left[cap : 2 * cap], from_right[3 * cap :]], axis=0
    )
    width = 6 * cap
    deep = -(-2 * width // 128) * 128
    gather2 = jnp.concatenate(
        [gather] * 2 + [jnp.zeros((deep - 2 * width, pipes), f32)], axis=0
    )
    spread_in = (PENALTY * gather2.T).astype(bf16)
    onward = dot(reach_out, spread_in).astype(bf16)
    tall = -(-(juncs + 2 * cap) // 128) * 128
    rest = jnp.zeros((tall - juncs - 2 * cap, pipes), f32)
    left_side = jnp.concatenate([incidence, lower, upper, rest], axis=0).T
    right_side = jnp.concatenate(
        [incidence, from_left[3 * cap :], from_right[cap : 2 * cap], rest], axis=0
    )
    local = (
        PENALTY * dot(left_side.astype(bf16), right_side.astype(bf16))
    ).astype(bf16)
    local2 = jnp.concatenate([local] * 2, axis=1)
    back = (PENALTY * left_side).astype(bf16)
    empty = jnp.zeros((tall - juncs, length), bf16)
    wanted = jnp.concatenate([wanted[:juncs], empty, wanted[juncs:], empty], axis=0)
    tail_rows = jnp.zeros((deep - 2 * width, length), bf16)

    def received(r):
        arrived(row_copies(r))
        return jnp.concatenate(split2(incoming[r]) + (tail_rows,), axis=0)

    def send(r, rows):
        outgoing[r] = rows
        start(row_copies(r))

    def near(field):
        pieces = split2(field)
        here = dot(local2, jnp.concatenate(pieces, axis=0))
        filtered = forward(*pieces)
        return here + backward(weight[...] * filtered) * inverse2

    def rows_of(field):
        return dot(reach_out2, cut2(field))

    at = lax.broadcasted_iota(jnp.int32, (1, 128), 1)

    def share(i, values):
        mine = jnp.zeros((1, 128), f32)
        for k, value in enumerate(values):
            mine = jnp.where(at == k, value, mine)
        part[i] = mine
        for slot, peer in others():
            pltpu.make_async_remote_copy(
                src_ref=part.at[i],
                dst_ref=parts.at[i, slot],
                send_sem=sum_send.at[i],
                recv_sem=sum_recv.at[i],
                device_id=peer,
                device_id_type=MESH,
            ).start()

    def whole(sem, i):
        pltpu.make_async_copy(parts.at[i], parts.at[i], sem.at[i]).wait()

    def shared(i, count):
        whole(sum_recv, i)
        sums = part[i] + jnp.sum(parts[i], axis=0)
        return [sums[:, k : k + 1] for k in range(count)]

    here = near_part + dot(jnp.concatenate([back] * 2, axis=1), wanted)
    here = here - dot(local2, prior_cut)
    rows = rows_of(here)
    came = received(0)
    send(1, rows - dot(onward, came))
    start0 = here - dot(spread_in, came)
    basis[0] = start0
    square = total(start0 * start0)
    here = near(start0)
    rows = rows_of(here)
    came = received(1)
    send(2, rows + dot(onward, came))
    image0 = here + dot(spread_in, came)
    share(0, [square, total(start0 * image0)])
    here = near(image0)
    rows = rows_of(here)
    came = received(2)
    rows = rows + dot(onward, came)
    square, curve = shared(0, 2)
    first = square / curve
    send(3, first * (outgoing[2] - first * rows))
    image00 = here + dot(spread_in, came)
    start0 = basis[0]
    after = start0 - first * image0
    image = first * (image0 - first * image00)
    basis[1] = after
    basis[2] = image
    pairs = ((start0, after), (start0, image), (after, after), (after, image), (image, image))
    known = [total(x * y) for x, y in pairs]
    here = near(image)
    came = received(3)
    image2 = first * (here + dot(spread_in, came))
    basis[3] = image2
    share(1, known + [total(x * image2) for x in (basis[0], basis[1], basis[2])])
    for r in range(ITERS + 1):
        left_here(row_copies(r))
    left_here(pair_copies())
    whole(sum_send, 0)
    sa, si, aa, ai, ii, sj, aj, ij = shared(1, 8)
    whole(sum_send, 1)
    gram = ((square, sa, si, sj), (sa, aa, ai, aj), (si, ai, ii, ij))

    def product(a, b):
        out = None
        for i in range(4):
            for j in range(4):
                if i < 3 or j < 3:
                    term = a[i] * b[j] * (gram[i][j] if i < 3 else gram[j][i])
                    out = term if out is None else out + term
        return out

    zero = jnp.zeros((1, 1), f32)
    one = jnp.ones((1, 1), f32)
    remaining = [zero, one, zero, zero]
    now = aa
    direction = [now / square, one, zero, zero]
    moved = [one, zero, zero, zero]
    for i in range(1, ITERS):
        applied = [direction[0], -direction[0], direction[1], direction[2]]
        step = now / product(direction, applied)
        moved = [x + step * y for x, y in zip(moved, direction)]
        remaining = [x - step * y for x, y in zip(remaining, applied)]
        if i + 1 < ITERS:
            later = product(remaining, remaining)
            direction = [x + later / now * y for x, y in zip(remaining, direction)]
            now = later
    flows, residual = prior_ref[...], remaining[3] * basis[3]
    for i in range(3):
        flows = flows + first * moved[i] * basis[i]
        residual = residual + remaining[i] * basis[i]
    flows_ref[...] = flows
    residual_ref[...] = residual


def shards(nets, hours, *args):
    prior, demand, pipe = args[1], args[2], args[7]
    pipes, length = prior.shape
    cap = pipe.shape[2]
    args = [x.reshape(1, -1) if x.ndim == 1 else x for x in args]
    args = [pltpu.with_memory_space_constraint(x, pltpu.HBM) for x in args]
    vmem = pl.BlockSpec(memory_space=pltpu.VMEM)
    rounds = ITERS + 1
    field = jax.ShapeDtypeStruct(prior.shape, f32)
    return pl.pallas_call(
        functools.partial(kernel, nets, hours),
        out_shape=(field, field),
        in_specs=[pl.BlockSpec(memory_space=pltpu.HBM)] * 10,
        out_specs=(vmem, vmem),
        scratch_shapes=[pltpu.VMEM(x.shape, x.dtype) for x in args[:7]]
        + [pltpu.SMEM(x.shape, x.dtype) for x in args[7:]]
        + [
            pltpu.SemaphoreType.DMA((10,)),
            pltpu.VMEM((pipes, length), f32),
            pltpu.VMEM((4, 3 * (length // 2), length // 2), bf16),
            pltpu.VMEM((rounds, 4 * cap, length), f32),
            pltpu.VMEM((rounds, 6 * cap, length), f32),
            pltpu.VMEM((4 * cap, 128), f32),
            pltpu.VMEM((2, 4 * cap, 128), f32),
            pltpu.VMEM((rounds, pipes, length), f32),
            pltpu.VMEM((2, 1, 128), f32),
            pltpu.VMEM((2, nets * hours - 1, 1, 128), f32),
            pltpu.SemaphoreType.DMA((rounds, 4)),
            pltpu.SemaphoreType.DMA((rounds, 4)),
            pltpu.SemaphoreType.DMA((2,)),
            pltpu.SemaphoreType.DMA((2,)),
            pltpu.SemaphoreType.DMA((2,)),
            pltpu.SemaphoreType.DMA((2,)),
        ],
        compiler_params=pltpu.CompilerParams(
            collective_id=0, has_side_effects=True, vmem_limit_bytes=32 * 2**20
        ),
        cost_estimate=pl.CostEstimate(
            flops=3 * 8 * 2 * pipes * length * length,
            bytes_accessed=5 * 4 * pipes * length,
            transcendentals=0,
        ),
    )(*args)

def solution(mesh):
    placed = (
        P("net", "hour"),
        P("net", "hour"),
        P("net", "hour"),
        P("net"),
        P(),
        P("net"),
        P("net"),
        P("net", None, None),
        P("net", None),
        P("net", None, None),
    )
    return jax.shard_map(
        functools.partial(shards, mesh.shape["net"], mesh.shape["hour"]),
        mesh=mesh,
        in_specs=placed,
        out_specs=(P("net", "hour"), P("net", "hour")),
        check_vma=False,
    )
```

```python
import functools

import jax
import jax.numpy as jnp
from jax import lax
from jax.experimental import pallas as pl
from jax.experimental.pallas import tpu as pltpu
from jax.sharding import PartitionSpec as P

ITERS = 3
EDGE = 1.5
PENALTY = 4.0
MESH = pl.DeviceIdType.MESH
f32 = jnp.float32
bf16 = jnp.bfloat16


def dot(a, b):
    return jnp.dot(a, b, preferred_element_type=f32)


def split2(x):
    high = x.astype(bf16)
    return high, (x - high.astype(f32)).astype(bf16)


def cut2(x):
    return jnp.concatenate(split2(x), axis=0)


def total(x):
    return jnp.sum(jnp.sum(x, axis=0, keepdims=True), axis=1, keepdims=True)


def halves(x):
    half = x.shape[1] // 2
    return jnp.concatenate([x[:, :half], x[:, half:]], axis=0)


def joined(x):
    half = x.shape[0] // 2
    return jnp.concatenate([x[:half], x[half:]], axis=1)


def kernel(
    nets,
    hours,
    *refs,
):
    given, refs = refs[:10], refs[10:]
    flows_ref, residual_ref = refs[:2]
    held, refs = refs[2:12], refs[12:]
    (
        measured_ref,
        prior_ref,
        demand_ref,
        sigma_ref,
        coef_ref,
        tail_ref,
        head_ref,
        pipe_ref,
        count_ref,
        arrival_ref,
    ) = held
    (
        load,
        weight,
        toep,
        outgoing,
        incoming,
        pairs_out,
        pairs_in,
        basis,
        part,
        parts,
        row_send,
        row_recv,
        pair_send,
        pair_recv,
        sum_send,
        sum_recv,
    ) = refs
    loads = [
        pltpu.make_async_copy(src, dst, load.at[i])
        for i, (src, dst) in enumerate(zip(given, held))
    ]
    for i in (9, 8, 7, 6, 5, 1, 2, 4, 3, 0):
        loads[i].start()

    pipes, length = prior_ref.shape
    juncs = demand_ref.shape[0]
    cap = pipe_ref.shape[2]
    half = length // 2
    net = lax.axis_index("net")
    hour = lax.axis_index("hour")
    has_left, has_right = net > 0, net < nets - 1
    has_left2, has_right2 = net > 1, net < nets - 2

    def clear(missing, ref):
        @pl.when(missing)
        def _():
            ref[...] = jnp.zeros(ref.shape, f32)

    for r in range(ITERS + 1):
        clear(net == 0, incoming.at[r, pl.ds(0, 2 * cap)])
        clear(net == nets - 1, incoming.at[r, pl.ds(2 * cap, 2 * cap)])
        clear(net < 2, incoming.at[r, pl.ds(4 * cap, cap)])
        clear(net >= nets - 2, incoming.at[r, pl.ds(5 * cap, cap)])
    clear(net == 0, pairs_in.at[0])
    clear(net == nets - 1, pairs_in.at[1])

    barrier = pltpu.get_barrier_semaphore()

    def others():
        for i in range(nets):
            for j in range(hours):
                if i + j > 0:
                    far_net = jnp.where(net + i >= nets, net + i - nets, net + i)
                    far_hour = jnp.where(hour + j >= hours, hour + j - hours, hour + j)
                    yield i * hours + j - 1, (far_net, far_hour)

    for _, peer in others():
        pl.semaphore_signal(barrier, inc=1, device_id=peer, device_id_type=MESH)
    for i in (9, 8, 7, 6, 5):
        loads[i].wait()

    slots = 4 * cap
    sub = lax.broadcasted_iota(jnp.int32, (slots, pipes), 0)
    lane = lax.broadcasted_iota(jnp.int32, (slots, pipes), 1)
    target = jnp.full((slots, pipes), -1, jnp.int32)
    for s in range(2):
        live = count_ref[0, s]
        for k in range(cap):
            own = jnp.where(k < live, pipe_ref[0, s, k], -1)
            target = jnp.where(sub == 2 * s * cap + k, own, target)
    chosen = (lane == target).astype(f32)
    sub_j = lax.broadcasted_iota(jnp.int32, (slots, juncs), 0)
    lane_j = lax.broadcasted_iota(jnp.int32, (slots, juncs), 1)
    landing_at = jnp.full((slots, juncs), -1, jnp.int32)
    for s in range(2):
        for k in range(cap):
            landing_at = jnp.where(
                sub_j == (2 * s + 1) * cap + k, arrival_ref[0, s, k], landing_at
            )
    landing = (lane_j == landing_at).astype(f32)
    interior = 1.0 - jnp.sum(chosen, axis=0, keepdims=True)
    junction = lax.broadcasted_iota(jnp.int32, (juncs, pipes), 0)
    incidence = (junction == head_ref[...]).astype(f32) * interior - (
        junction == tail_ref[...]
    ).astype(f32)
    landing16 = landing.astype(bf16)
    reach = chosen + dot(landing16, incidence.astype(bf16))

    def swapped(x):
        return jnp.concatenate(
            [
                x[cap : 2 * cap],
                x[:cap],
                x[3 * cap :],
                x[2 * cap : 3 * cap],
            ],
            axis=0,
        )

    reach_out = swapped(reach).astype(bf16)
    reach_out2 = jnp.concatenate([reach_out] * 2, axis=1)
    landing_out = swapped(landing).astype(bf16)
    pad_l = jnp.concatenate([landing, jnp.zeros((128 - slots, juncs), f32)], axis=0)
    pairs_out[...] = lax.dot_general(
        landing16,
        pad_l.astype(bf16),
        (((1,), (1,)), ((), ())),
        preferred_element_type=f32,
    )

    loads[1].wait()
    loads[2].wait()
    prior = prior_ref[...]
    prior_cut = cut2(prior)
    wanted = cut2(demand_ref[...])
    outgoing[0] = dot(reach_out2, prior_cut) - dot(
        jnp.concatenate([landing_out] * 2, axis=1), wanted
    )
    pl.semaphore_wait(barrier, nets * hours - 1)

    def remote(src, dst, send, recv, shift):
        return pltpu.make_async_remote_copy(
            src_ref=src,
            dst_ref=dst,
            send_sem=send,
            recv_sem=recv,
            device_id=(net + shift, hour),
            device_id_type=MESH,
        )

    def pair_copies():
        yield has_right, has_left, remote(
            pairs_out, pairs_in.at[0], pair_send.at[0], pair_recv.at[0], 1
        )
        yield has_left, has_right, remote(
            pairs_out, pairs_in.at[1], pair_send.at[1], pair_recv.at[1], -1
        )

    def row_copies(r):
        def one(i, start, size, dest, shift):
            return remote(
                outgoing.at[r, pl.ds(start, size)],
                incoming.at[r, pl.ds(dest, size)],
                row_send.at[r, i],
                row_recv.at[r, i],
                shift,
            )

        yield has_right, has_left, one(0, 2 * cap, 2 * cap, 0, 1)
        yield has_left, has_right, one(1, 0, 2 * cap, 2 * cap, -1)
        yield has_right2, has_left2, one(2, 3 * cap, cap, 4 * cap, 2)
        yield has_left2, has_right2, one(3, cap, cap, 5 * cap, -2)

    def start(copies):
        for sends, _, copy in copies:

            @pl.when(sends)
            def _():
                copy.start()

    def arrived(copies):
        for _, receives, copy in copies:

            @pl.when(receives)
            def _():
                copy.wait_recv()

    def left_here(copies):
        for sends, _, copy in copies:

            @pl.when(sends)
            def _():
                copy.wait_send()

    start(pair_copies())
    start(row_copies(0))
    loads[4].wait()

    spread = jnp.broadcast_to(coef_ref[...], (half, length))
    rolled = pltpu.roll(spread, 0, 1, stride=1, stride_axis=0)
    at_row = lax.broadcasted_iota(jnp.int32, (half, half), 0)
    at_col = lax.broadcasted_iota(jnp.int32, (half, half), 1)
    near = jnp.where(at_col >= at_row, rolled[:, :half], 0.0)
    far = rolled[:, half:]
    for i, block in enumerate((near, far, near.T, far.T)):
        high, low = split2(block)
        toep[i, pl.ds(0, half)] = high
        toep[i, pl.ds(half, half)] = high
        toep[i, pl.ds(2 * half, half)] = low


    def thrice(high, low, i):
        return dot(jnp.concatenate([high, low, high], axis=1), toep[i])

    def forward(high, low):
        high, low = halves(high), halves(low)
        same = thrice(high, low, 0)
        cross = thrice(high[:pipes], low[:pipes], 1)
        return jnp.concatenate([same[:pipes], same[pipes:] + cross], axis=1)

    def backward(field):
        high, low = split2(halves(field))
        same = thrice(high, low, 2)
        cross = thrice(high[pipes:], low[pipes:], 3)
        return jnp.concatenate([same[:pipes] + cross, same[pipes:]], axis=1)

    loads[3].wait()
    loads[0].wait()
    eye = lax.broadcasted_iota(jnp.int32, (pipes, pipes), 0) == (
        lax.broadcasted_iota(jnp.int32, (pipes, pipes), 1)
    )
    sigma = jnp.sum(jnp.where(eye, sigma_ref[...], 0.0), axis=1, keepdims=True)
    inverse = 1.0 / sigma
    inverse2 = inverse * inverse
    whitened = forward(*split2((measured_ref[...] - prior) * inverse))
    huber = EDGE / jnp.maximum(jnp.abs(whitened), EDGE)
    weight[...] = huber
    near_part = backward(huber * whitened * sigma) * inverse2

    arrived(pair_copies())
    zero = jnp.zeros((cap, pipes), f32)
    fill = jnp.zeros((128 - slots, pipes), f32)
    lower = chosen[:cap]
    upper = chosen[2 * cap : 3 * cap]
    lower_at = jnp.concatenate([zero, zero, zero, lower, fill], axis=0)
    upper_at = jnp.concatenate([zero, upper, zero, zero, fill], axis=0)
    from_left = dot(pairs_in[0].astype(bf16), lower_at.astype(bf16))
    from_right = dot(pairs_in[1].astype(bf16), upper_at.astype(bf16))
    gather = jnp.concatenate(
        [reach, from_left[cap : 2 * cap], from_right[3 * cap :]], axis=0
    )
    width = 6 * cap
    deep = -(-2 * width // 128) * 128
    gather2 = jnp.concatenate(
        [gather] * 2 + [jnp.zeros((deep - 2 * width, pipes), f32)], axis=0
    )
    spread_in = (PENALTY * gather2.T).astype(bf16)
    onward = dot(reach_out, spread_in).astype(bf16)
    gather_both = jnp.concatenate([PENALTY * gather] * 2, axis=1).astype(bf16)
    tall = -(-(juncs + 2 * cap) // 128) * 128
    rest = jnp.zeros((tall - juncs - 2 * cap, pipes), f32)
    left_side = jnp.concatenate([incidence, lower, upper, rest], axis=0).T
    right_side = jnp.concatenate(
        [incidence, from_left[3 * cap :], from_right[cap : 2 * cap], rest], axis=0
    )
    local = (
        PENALTY * dot(left_side.astype(bf16), right_side.astype(bf16))
    ).astype(bf16)
    local2 = jnp.concatenate([local] * 2, axis=1)
    back = (PENALTY * left_side).astype(bf16)
    empty = jnp.zeros((tall - juncs, length), bf16)
    wanted = jnp.concatenate([wanted[:juncs], empty, wanted[juncs:], empty], axis=0)
    tail_rows = jnp.zeros((deep - 2 * width, length), bf16)

    def cut_rows(x):
        return jnp.concatenate(split2(x) + (tail_rows,), axis=0)

    def received(r):
        arrived(row_copies(r))
        return cut_rows(incoming[r])

    def send(r, rows):
        outgoing[r] = rows
        start(row_copies(r))

    def near(field):
        pieces = split2(field)
        cut = jnp.concatenate(pieces, axis=0)
        here = dot(local2, cut)
        filtered = forward(*pieces)
        return here + backward(weight[...] * filtered) * inverse2, cut

    def rows_of(field):
        return dot(reach_out2, cut2(field))

    at = lax.broadcasted_iota(jnp.int32, (1, 128), 1)

    def share(i, values):
        mine = jnp.zeros((1, 128), f32)
        for k, value in enumerate(values):
            mine = jnp.where(at == k, value, mine)
        part[i] = mine
        for slot, peer in others():
            pltpu.make_async_remote_copy(
                src_ref=part.at[i],
                dst_ref=parts.at[i, slot],
                send_sem=sum_send.at[i],
                recv_sem=sum_recv.at[i],
                device_id=peer,
                device_id_type=MESH,
            ).start()

    def whole(sem, i):
        pltpu.make_async_copy(parts.at[i], parts.at[i], sem.at[i]).wait()

    def shared(i, count):
        whole(sum_recv, i)
        sums = part[i] + jnp.sum(parts[i], axis=0)
        return [sums[:, k : k + 1] for k in range(count)]

    here = near_part + dot(jnp.concatenate([back] * 2, axis=1), wanted)
    here = here - dot(local2, prior_cut)
    rows = rows_of(here)
    came = received(0)
    send(1, rows - dot(onward, came))
    start0 = here - dot(spread_in, came)
    basis[0] = start0
    square = total(start0 * start0)
    here, _ = near(start0)
    rows = rows_of(here)
    came = received(1)
    send(2, rows + dot(onward, came))
    image0 = here + dot(spread_in, came)
    share(0, [square, total(start0 * image0)])
    here, _ = near(image0)
    rows = rows_of(here)
    came = received(2)
    send(3, rows + dot(onward, came))
    image00 = here + dot(spread_in, came)
    square, curve = shared(0, 2)
    first = square / curve
    start0 = basis[0]
    after = start0 - first * image0
    image = first * (image0 - first * image00)
    basis[1] = after
    basis[2] = image
    pairs = ((start0, after), (start0, image), (after, after), (after, image), (image, image))
    known = [total(x * y) for x, y in pairs]
    here, cut = near(image)
    taken = dot(gather_both, cut)
    local_part = total(image * here)
    arrived(row_copies(3))
    came = first * (incoming[2] - first * incoming[3])
    share(1, known + [first * (local_part + total(taken * came))])
    basis[3] = first * (here + dot(spread_in, cut_rows(came)))
    for r in range(ITERS + 1):
        left_here(row_copies(r))
    left_here(pair_copies())
    whole(sum_send, 0)
    sa, si, aa, ai, ii, ij = shared(1, 6)
    sj, aj = si - ai, ii
    whole(sum_send, 1)
    gram = ((square, sa, si, sj), (sa, aa, ai, aj), (si, ai, ii, ij))

    def product(a, b):
        out = None
        for i in range(4):
            for j in range(4):
                if i < 3 or j < 3:
                    term = a[i] * b[j] * (gram[i][j] if i < 3 else gram[j][i])
                    out = term if out is None else out + term
        return out

    zero = jnp.zeros((1, 1), f32)
    one = jnp.ones((1, 1), f32)
    remaining = [zero, one, zero, zero]
    now = aa
    direction = [now / square, one, zero, zero]
    moved = [one, zero, zero, zero]
    for i in range(1, ITERS):
        applied = [direction[0], -direction[0], direction[1], direction[2]]
        step = now / product(direction, applied)
        moved = [x + step * y for x, y in zip(moved, direction)]
        remaining = [x - step * y for x, y in zip(remaining, applied)]
        if i + 1 < ITERS:
            later = product(remaining, remaining)
            direction = [x + later / now * y for x, y in zip(remaining, direction)]
            now = later
    flows, residual = prior_ref[...], remaining[3] * basis[3]
    for i in range(3):
        flows = flows + first * moved[i] * basis[i]
        residual = residual + remaining[i] * basis[i]
    flows_ref[...] = flows
    residual_ref[...] = residual


def shards(nets, hours, *args):
    prior, demand, pipe = args[1], args[2], args[7]
    pipes, length = prior.shape
    cap = pipe.shape[2]
    args = [x.reshape(1, -1) if x.ndim == 1 else x for x in args]
    args = [pltpu.with_memory_space_constraint(x, pltpu.HBM) for x in args]
    vmem = pl.BlockSpec(memory_space=pltpu.VMEM)
    rounds = ITERS + 1
    field = jax.ShapeDtypeStruct(prior.shape, f32)
    return pl.pallas_call(
        functools.partial(kernel, nets, hours),
        out_shape=(field, field),
        in_specs=[pl.BlockSpec(memory_space=pltpu.HBM)] * 10,
        out_specs=(vmem, vmem),
        scratch_shapes=[pltpu.VMEM(x.shape, x.dtype) for x in args[:7]]
        + [pltpu.SMEM(x.shape, x.dtype) for x in args[7:]]
        + [
            pltpu.SemaphoreType.DMA((10,)),
            pltpu.VMEM((pipes, length), f32),
            pltpu.VMEM((4, 3 * (length // 2), length // 2), bf16),
            pltpu.VMEM((rounds, 4 * cap, length), f32),
            pltpu.VMEM((rounds, 6 * cap, length), f32),
            pltpu.VMEM((4 * cap, 128), f32),
            pltpu.VMEM((2, 4 * cap, 128), f32),
            pltpu.VMEM((rounds, pipes, length), f32),
            pltpu.VMEM((2, 1, 128), f32),
            pltpu.VMEM((2, nets * hours - 1, 1, 128), f32),
            pltpu.SemaphoreType.DMA((rounds, 4)),
            pltpu.SemaphoreType.DMA((rounds, 4)),
            pltpu.SemaphoreType.DMA((2,)),
            pltpu.SemaphoreType.DMA((2,)),
            pltpu.SemaphoreType.DMA((2,)),
            pltpu.SemaphoreType.DMA((2,)),
        ],
        compiler_params=pltpu.CompilerParams(
            collective_id=0, has_side_effects=True, vmem_limit_bytes=32 * 2**20
        ),
        cost_estimate=pl.CostEstimate(
            flops=3 * 8 * 2 * pipes * length * length,
            bytes_accessed=5 * 4 * pipes * length,
            transcendentals=0,
        ),
    )(*args)

def solution(mesh):
    placed = (
        P("net", "hour"),
        P("net", "hour"),
        P("net", "hour"),
        P("net"),
        P(),
        P("net"),
        P("net"),
        P("net", None, None),
        P("net", None),
        P("net", None, None),
    )
    return jax.shard_map(
        functools.partial(shards, mesh.shape["net"], mesh.shape["hour"]),
        mesh=mesh,
        in_specs=placed,
        out_specs=(P("net", "hour"), P("net", "hour")),
        check_vma=False,
    )
```

```python
import functools

import jax
import jax.numpy as jnp
from jax import lax
from jax.experimental import pallas as pl
from jax.experimental.pallas import tpu as pltpu
from jax.sharding import PartitionSpec as P

ITERS = 3
EDGE = 1.5
PENALTY = 4.0
MESH = pl.DeviceIdType.MESH
f32 = jnp.float32
bf16 = jnp.bfloat16


def dot(a, b):
    return jnp.dot(a, b, preferred_element_type=f32)


def split2(x):
    high = x.astype(bf16)
    return high, (x - high.astype(f32)).astype(bf16)


def cut2(x):
    return jnp.concatenate(split2(x), axis=0)


def total(x):
    return jnp.sum(jnp.sum(x, axis=0, keepdims=True), axis=1, keepdims=True)


def halves(x):
    half = x.shape[1] // 2
    return jnp.concatenate([x[:, :half], x[:, half:]], axis=0)


def joined(x):
    half = x.shape[0] // 2
    return jnp.concatenate([x[:half], x[half:]], axis=1)


def kernel(
    nets,
    hours,
    *refs,
):
    given, refs = refs[:10], refs[10:]
    flows_ref, residual_ref = refs[:2]
    held, refs = refs[2:12], refs[12:]
    (
        measured_ref,
        prior_ref,
        demand_ref,
        sigma_ref,
        coef_ref,
        tail_ref,
        head_ref,
        pipe_ref,
        count_ref,
        arrival_ref,
    ) = held
    (
        load,
        weight,
        toep,
        outgoing,
        incoming,
        pairs_out,
        pairs_in,
        basis,
        part,
        parts_hour,
        parts_net,
        parts,
        row_send,
        row_recv,
        pair_send,
        pair_recv,
        sum_send,
        sum_recv,
    ) = refs
    loads = [
        pltpu.make_async_copy(src, dst, load.at[i])
        for i, (src, dst) in enumerate(zip(given, held))
    ]
    for i in (9, 8, 7, 6, 5, 1, 2, 4, 3, 0):
        loads[i].start()

    pipes, length = prior_ref.shape
    juncs = demand_ref.shape[0]
    cap = pipe_ref.shape[2]
    half = length // 2
    net = lax.axis_index("net")
    hour = lax.axis_index("hour")
    has_left, has_right = net > 0, net < nets - 1
    has_left2, has_right2 = net > 1, net < nets - 2

    def clear(missing, ref):
        @pl.when(missing)
        def _():
            ref[...] = jnp.zeros(ref.shape, f32)

    for r in range(ITERS + 1):
        clear(net == 0, incoming.at[r, pl.ds(0, 2 * cap)])
        clear(net == nets - 1, incoming.at[r, pl.ds(2 * cap, 2 * cap)])
        clear(net < 2, incoming.at[r, pl.ds(4 * cap, cap)])
        clear(net >= nets - 2, incoming.at[r, pl.ds(5 * cap, cap)])
    clear(net == 0, pairs_in.at[0])
    clear(net == nets - 1, pairs_in.at[1])

    barrier = pltpu.get_barrier_semaphore()

    def others():
        for i in range(nets):
            for j in range(hours):
                if i + j > 0:
                    far_net = jnp.where(net + i >= nets, net + i - nets, net + i)
                    far_hour = jnp.where(hour + j >= hours, hour + j - hours, hour + j)
                    yield i * hours + j - 1, (far_net, far_hour)

    for _, peer in others():
        pl.semaphore_signal(barrier, inc=1, device_id=peer, device_id_type=MESH)
    for i in (9, 8, 7, 6, 5):
        loads[i].wait()

    slots = 4 * cap
    sub = lax.broadcasted_iota(jnp.int32, (slots, pipes), 0)
    lane = lax.broadcasted_iota(jnp.int32, (slots, pipes), 1)
    target = jnp.full((slots, pipes), -1, jnp.int32)
    for s in range(2):
        live = count_ref[0, s]
        for k in range(cap):
            own = jnp.where(k < live, pipe_ref[0, s, k], -1)
            target = jnp.where(sub == 2 * s * cap + k, own, target)
    chosen = (lane == target).astype(f32)
    sub_j = lax.broadcasted_iota(jnp.int32, (slots, juncs), 0)
    lane_j = lax.broadcasted_iota(jnp.int32, (slots, juncs), 1)
    landing_at = jnp.full((slots, juncs), -1, jnp.int32)
    for s in range(2):
        for k in range(cap):
            landing_at = jnp.where(
                sub_j == (2 * s + 1) * cap + k, arrival_ref[0, s, k], landing_at
            )
    landing = (lane_j == landing_at).astype(f32)
    interior = 1.0 - jnp.sum(chosen, axis=0, keepdims=True)
    junction = lax.broadcasted_iota(jnp.int32, (juncs, pipes), 0)
    incidence = (junction == head_ref[...]).astype(f32) * interior - (
        junction == tail_ref[...]
    ).astype(f32)
    landing16 = landing.astype(bf16)
    reach = chosen + dot(landing16, incidence.astype(bf16))

    def swapped(x):
        return jnp.concatenate(
            [
                x[cap : 2 * cap],
                x[:cap],
                x[3 * cap :],
                x[2 * cap : 3 * cap],
            ],
            axis=0,
        )

    reach_out = swapped(reach).astype(bf16)
    reach_out2 = jnp.concatenate([reach_out] * 2, axis=1)
    landing_out = swapped(landing).astype(bf16)
    pad_l = jnp.concatenate([landing, jnp.zeros((128 - slots, juncs), f32)], axis=0)
    pairs_out[...] = lax.dot_general(
        landing16,
        pad_l.astype(bf16),
        (((1,), (1,)), ((), ())),
        preferred_element_type=f32,
    )

    loads[1].wait()
    loads[2].wait()
    prior = prior_ref[...]
    prior_cut = cut2(prior)
    wanted = cut2(demand_ref[...])
    outgoing[0] = dot(reach_out2, prior_cut) - dot(
        jnp.concatenate([landing_out] * 2, axis=1), wanted
    )
    pl.semaphore_wait(barrier, nets * hours - 1)

    def remote(src, dst, send, recv, shift):
        return pltpu.make_async_remote_copy(
            src_ref=src,
            dst_ref=dst,
            send_sem=send,
            recv_sem=recv,
            device_id=(net + shift, hour),
            device_id_type=MESH,
        )

    def pair_copies():
        yield has_right, has_left, remote(
            pairs_out, pairs_in.at[0], pair_send.at[0], pair_recv.at[0], 1
        )
        yield has_left, has_right, remote(
            pairs_out, pairs_in.at[1], pair_send.at[1], pair_recv.at[1], -1
        )

    def row_copies(r):
        def one(i, start, size, dest, shift):
            return remote(
                outgoing.at[r, pl.ds(start, size)],
                incoming.at[r, pl.ds(dest, size)],
                row_send.at[r, i],
                row_recv.at[r, i],
                shift,
            )

        yield has_right, has_left, one(0, 2 * cap, 2 * cap, 0, 1)
        yield has_left, has_right, one(1, 0, 2 * cap, 2 * cap, -1)
        yield has_right2, has_left2, one(2, 3 * cap, cap, 4 * cap, 2)
        yield has_left2, has_right2, one(3, cap, cap, 5 * cap, -2)

    def start(copies):
        for sends, _, copy in copies:

            @pl.when(sends)
            def _():
                copy.start()

    def arrived(copies):
        for _, receives, copy in copies:

            @pl.when(receives)
            def _():
                copy.wait_recv()

    def left_here(copies):
        for sends, _, copy in copies:

            @pl.when(sends)
            def _():
                copy.wait_send()

    start(row_copies(0))
    start(pair_copies())
    loads[4].wait()

    spread = jnp.broadcast_to(coef_ref[...], (half, length))
    rolled = pltpu.roll(spread, 0, 1, stride=1, stride_axis=0)
    at_row = lax.broadcasted_iota(jnp.int32, (half, half), 0)
    at_col = lax.broadcasted_iota(jnp.int32, (half, half), 1)
    near = jnp.where(at_col >= at_row, rolled[:, :half], 0.0)
    far = rolled[:, half:]
    for i, block in enumerate((near, far, near.T, far.T)):
        high, low = split2(block)
        toep[i, pl.ds(0, half)] = high
        toep[i, pl.ds(half, half)] = high
        toep[i, pl.ds(2 * half, half)] = low


    def thrice(high, low, i):
        return dot(jnp.concatenate([high, low, high], axis=1), toep[i])

    def forward(high, low):
        high, low = halves(high), halves(low)
        same = thrice(high, low, 0)
        cross = thrice(high[:pipes], low[:pipes], 1)
        return jnp.concatenate([same[:pipes], same[pipes:] + cross], axis=1)

    def backward(field):
        high, low = split2(halves(field))
        same = thrice(high, low, 2)
        cross = thrice(high[pipes:], low[pipes:], 3)
        return jnp.concatenate([same[:pipes] + cross, same[pipes:]], axis=1)

    loads[3].wait()
    loads[0].wait()
    eye = lax.broadcasted_iota(jnp.int32, (pipes, pipes), 0) == (
        lax.broadcasted_iota(jnp.int32, (pipes, pipes), 1)
    )
    sigma = jnp.sum(jnp.where(eye, sigma_ref[...], 0.0), axis=1, keepdims=True)
    inverse = 1.0 / sigma
    inverse2 = inverse * inverse
    whitened = forward(*split2((measured_ref[...] - prior) * inverse))
    huber = EDGE / jnp.maximum(jnp.abs(whitened), EDGE)
    weight[...] = huber
    near_part = backward(huber * whitened * sigma) * inverse2

    arrived(pair_copies())
    zero = jnp.zeros((cap, pipes), f32)
    fill = jnp.zeros((128 - slots, pipes), f32)
    lower = chosen[:cap]
    upper = chosen[2 * cap : 3 * cap]
    lower_at = jnp.concatenate([zero, zero, zero, lower, fill], axis=0)
    upper_at = jnp.concatenate([zero, upper, zero, zero, fill], axis=0)
    from_left = dot(pairs_in[0].astype(bf16), lower_at.astype(bf16))
    from_right = dot(pairs_in[1].astype(bf16), upper_at.astype(bf16))
    gather = jnp.concatenate(
        [reach, from_left[cap : 2 * cap], from_right[3 * cap :]], axis=0
    )
    width = 6 * cap
    deep = -(-2 * width // 128) * 128
    gather2 = jnp.concatenate(
        [gather] * 2 + [jnp.zeros((deep - 2 * width, pipes), f32)], axis=0
    )
    spread_in = (PENALTY * gather2.T).astype(bf16)
    onward = dot(reach_out, spread_in).astype(bf16)
    gather_both = jnp.concatenate([PENALTY * gather] * 2, axis=1).astype(bf16)
    tall = -(-(juncs + 2 * cap) // 128) * 128
    rest = jnp.zeros((tall - juncs - 2 * cap, pipes), f32)
    left_side = jnp.concatenate([incidence, lower, upper, rest], axis=0).T
    right_side = jnp.concatenate(
        [incidence, from_left[3 * cap :], from_right[cap : 2 * cap], rest], axis=0
    )
    local = (
        PENALTY * dot(left_side.astype(bf16), right_side.astype(bf16))
    ).astype(bf16)
    local2 = jnp.concatenate([local] * 2, axis=1)
    back = (PENALTY * left_side).astype(bf16)
    empty = jnp.zeros((tall - juncs, length), bf16)
    wanted = jnp.concatenate([wanted[:juncs], empty, wanted[juncs:], empty], axis=0)
    tail_rows = jnp.zeros((deep - 2 * width, length), bf16)

    def cut_rows(x):
        return jnp.concatenate(split2(x) + (tail_rows,), axis=0)

    def received(r):
        arrived(row_copies(r))
        return cut_rows(incoming[r])

    def send(r, rows):
        outgoing[r] = rows
        start(row_copies(r))

    def near(field):
        pieces = split2(field)
        cut = jnp.concatenate(pieces, axis=0)
        here = dot(local2, cut)
        filtered = forward(*pieces)
        return here + backward(weight[...] * filtered) * inverse2, cut

    def rows_of(field):
        return dot(reach_out2, cut2(field))

    at = lax.broadcasted_iota(jnp.int32, (1, 128), 1)

    def row_of(values):
        mine = jnp.zeros((1, 128), f32)
        for k, value in enumerate(values):
            mine = jnp.where(at == k, value, mine)
        return mine

    def post(mine, theirs, peers, k):
        for slot, peer in peers:
            pltpu.make_async_remote_copy(
                src_ref=mine,
                dst_ref=theirs.at[slot],
                send_sem=sum_send.at[k],
                recv_sem=sum_recv.at[k],
                device_id=peer,
                device_id_type=MESH,
            ).start()

    def whole(theirs, sem):
        pltpu.make_async_copy(theirs, theirs, sem).wait()

    def added(mine, theirs, k):
        whole(theirs, sum_recv.at[k])
        return mine[...] + jnp.sum(theirs[...], axis=0)

    def ring(at, count):
        for i in range(1, count):
            yield i - 1, jnp.where(at + i >= count, at + i - count, at + i)

    hour_peers = [(slot, (net, far)) for slot, far in ring(hour, hours)]
    net_peers = [(slot, (far, hour)) for slot, far in ring(net, nets)]

    here = near_part + dot(jnp.concatenate([back] * 2, axis=1), wanted)
    here = here - dot(local2, prior_cut)
    rows = rows_of(here)
    came = received(0)
    send(1, rows - dot(onward, came))
    start0 = here - dot(spread_in, came)
    basis[0] = start0
    square = total(start0 * start0)
    here, _ = near(start0)
    rows = rows_of(here)
    came = received(1)
    send(2, rows + dot(onward, came))
    image0 = here + dot(spread_in, came)
    part[0] = row_of([square, total(start0 * image0)])
    post(part.at[0], parts_hour, hour_peers, 0)
    here, _ = near(image0)
    rows = rows_of(here)
    part[1] = added(part.at[0], parts_hour, 0)
    post(part.at[1], parts_net, net_peers, 1)
    came = received(2)
    send(3, rows + dot(onward, came))
    image00 = here + dot(spread_in, came)
    sums = added(part.at[1], parts_net, 1)
    square, curve = sums[:, :1], sums[:, 1:2]
    first = square / curve
    start0 = basis[0]
    after = start0 - first * image0
    image = first * (image0 - first * image00)
    basis[1] = after
    basis[2] = image
    pairs = ((start0, after), (start0, image), (after, after), (after, image), (image, image))
    known = [total(x * y) for x, y in pairs]
    here, cut = near(image)
    taken = dot(gather_both, cut)
    local_part = total(image * here)
    arrived(row_copies(3))
    came = first * (incoming[2] - first * incoming[3])
    part[2] = row_of(known + [first * (local_part + total(taken * came))])
    post(part.at[2], parts, others(), 2)
    basis[3] = first * (here + dot(spread_in, cut_rows(came)))
    for r in range(ITERS + 1):
        left_here(row_copies(r))
    left_here(pair_copies())
    whole(parts_hour, sum_send.at[0])
    whole(parts_net, sum_send.at[1])
    sums = added(part.at[2], parts, 2)
    sa, si, aa, ai, ii, ij = [sums[:, k : k + 1] for k in range(6)]
    sj, aj = si - ai, ii
    whole(parts, sum_send.at[2])
    gram = ((square, sa, si, sj), (sa, aa, ai, aj), (si, ai, ii, ij))

    def product(a, b):
        out = None
        for i in range(4):
            for j in range(4):
                if i < 3 or j < 3:
                    term = a[i] * b[j] * (gram[i][j] if i < 3 else gram[j][i])
                    out = term if out is None else out + term
        return out

    zero = jnp.zeros((1, 1), f32)
    one = jnp.ones((1, 1), f32)
    remaining = [zero, one, zero, zero]
    now = aa
    direction = [now / square, one, zero, zero]
    moved = [one, zero, zero, zero]
    for i in range(1, ITERS):
        applied = [direction[0], -direction[0], direction[1], direction[2]]
        step = now / product(direction, applied)
        moved = [x + step * y for x, y in zip(moved, direction)]
        remaining = [x - step * y for x, y in zip(remaining, applied)]
        if i + 1 < ITERS:
            later = product(remaining, remaining)
            direction = [x + later / now * y for x, y in zip(remaining, direction)]
            now = later
    flows, residual = prior_ref[...], remaining[3] * basis[3]
    for i in range(3):
        flows = flows + first * moved[i] * basis[i]
        residual = residual + remaining[i] * basis[i]
    flows_ref[...] = flows
    residual_ref[...] = residual


def shards(nets, hours, *args):
    prior, demand, pipe = args[1], args[2], args[7]
    pipes, length = prior.shape
    cap = pipe.shape[2]
    args = [x.reshape(1, -1) if x.ndim == 1 else x for x in args]
    args = [pltpu.with_memory_space_constraint(x, pltpu.HBM) for x in args]
    vmem = pl.BlockSpec(memory_space=pltpu.VMEM)
    rounds = ITERS + 1
    field = jax.ShapeDtypeStruct(prior.shape, f32)
    return pl.pallas_call(
        functools.partial(kernel, nets, hours),
        out_shape=(field, field),
        in_specs=[pl.BlockSpec(memory_space=pltpu.HBM)] * 10,
        out_specs=(vmem, vmem),
        scratch_shapes=[pltpu.VMEM(x.shape, x.dtype) for x in args[:7]]
        + [pltpu.SMEM(x.shape, x.dtype) for x in args[7:]]
        + [
            pltpu.SemaphoreType.DMA((10,)),
            pltpu.VMEM((pipes, length), f32),
            pltpu.VMEM((4, 3 * (length // 2), length // 2), bf16),
            pltpu.VMEM((rounds, 4 * cap, length), f32),
            pltpu.VMEM((rounds, 6 * cap, length), f32),
            pltpu.VMEM((4 * cap, 128), f32),
            pltpu.VMEM((2, 4 * cap, 128), f32),
            pltpu.VMEM((rounds, pipes, length), f32),
            pltpu.VMEM((3, 1, 128), f32),
            pltpu.VMEM((hours - 1, 1, 128), f32),
            pltpu.VMEM((nets - 1, 1, 128), f32),
            pltpu.VMEM((nets * hours - 1, 1, 128), f32),
            pltpu.SemaphoreType.DMA((rounds, 4)),
            pltpu.SemaphoreType.DMA((rounds, 4)),
            pltpu.SemaphoreType.DMA((2,)),
            pltpu.SemaphoreType.DMA((2,)),
            pltpu.SemaphoreType.DMA((3,)),
            pltpu.SemaphoreType.DMA((3,)),
        ],
        compiler_params=pltpu.CompilerParams(
            collective_id=0, has_side_effects=True, vmem_limit_bytes=32 * 2**20
        ),
        cost_estimate=pl.CostEstimate(
            flops=3 * 8 * 2 * pipes * length * length,
            bytes_accessed=5 * 4 * pipes * length,
            transcendentals=0,
        ),
    )(*args)

def solution(mesh):
    placed = (
        P("net", "hour"),
        P("net", "hour"),
        P("net", "hour"),
        P("net"),
        P(),
        P("net"),
        P("net"),
        P("net", None, None),
        P("net", None),
        P("net", None, None),
    )
    return jax.shard_map(
        functools.partial(shards, mesh.shape["net"], mesh.shape["hour"]),
        mesh=mesh,
        in_specs=placed,
        out_specs=(P("net", "hour"), P("net", "hour")),
        check_vma=False,
    )
```

```python
import functools

import jax
import jax.numpy as jnp
from jax import lax
from jax.experimental import pallas as pl
from jax.experimental.pallas import tpu as pltpu
from jax.sharding import PartitionSpec as P

ITERS = 3
EDGE = 1.5
PENALTY = 4.0
MESH = pl.DeviceIdType.MESH
f32 = jnp.float32
bf16 = jnp.bfloat16


def dot(a, b):
    return jnp.dot(a, b, preferred_element_type=f32)


def split2(x):
    high = x.astype(bf16)
    return high, (x - high.astype(f32)).astype(bf16)


def cut2(x):
    return jnp.concatenate(split2(x), axis=0)


def total(x):
    return jnp.sum(jnp.sum(x, axis=0, keepdims=True), axis=1, keepdims=True)


def halves(x):
    half = x.shape[1] // 2
    return jnp.concatenate([x[:, :half], x[:, half:]], axis=0)


def joined(x):
    half = x.shape[0] // 2
    return jnp.concatenate([x[:half], x[half:]], axis=1)


def kernel(
    nets,
    hours,
    *refs,
):
    given, refs = refs[:10], refs[10:]
    flows_ref, residual_ref = refs[:2]
    held, refs = refs[2:12], refs[12:]
    (
        measured_ref,
        prior_ref,
        demand_ref,
        sigma_ref,
        coef_ref,
        tail_ref,
        head_ref,
        pipe_ref,
        count_ref,
        arrival_ref,
    ) = held
    (
        load,
        weight,
        toep,
        outgoing,
        incoming,
        pairs_out,
        pairs_in,
        basis,
        part,
        parts,
        row_send,
        row_recv,
        pair_send,
        pair_recv,
        sum_send,
        sum_recv,
    ) = refs
    loads = [
        pltpu.make_async_copy(src, dst, load.at[i])
        for i, (src, dst) in enumerate(zip(given, held))
    ]
    for i in (9, 8, 7, 6, 5, 1, 2, 4, 3, 0):
        loads[i].start()

    pipes, length = prior_ref.shape
    juncs = demand_ref.shape[0]
    cap = pipe_ref.shape[2]
    half = length // 2
    net = lax.axis_index("net")
    hour = lax.axis_index("hour")
    has_left, has_right = net > 0, net < nets - 1
    has_left2, has_right2 = net > 1, net < nets - 2

    def clear(missing, ref):
        @pl.when(missing)
        def _():
            ref[...] = jnp.zeros(ref.shape, f32)

    for r in range(ITERS + 1):
        clear(net == 0, incoming.at[r, pl.ds(0, 2 * cap)])
        clear(net == nets - 1, incoming.at[r, pl.ds(2 * cap, 2 * cap)])
        clear(net < 2, incoming.at[r, pl.ds(4 * cap, cap)])
        clear(net >= nets - 2, incoming.at[r, pl.ds(5 * cap, cap)])
    clear(net == 0, pairs_in.at[0])
    clear(net == nets - 1, pairs_in.at[1])

    barrier = pltpu.get_barrier_semaphore()

    def others():
        for i in reversed(range(nets)):
            for j in reversed(range(hours)):
                if i + j > 0:
                    far_net = jnp.where(net + i >= nets, net + i - nets, net + i)
                    far_hour = jnp.where(hour + j >= hours, hour + j - hours, hour + j)
                    yield i * hours + j - 1, (far_net, far_hour)

    for _, peer in others():
        pl.semaphore_signal(barrier, inc=1, device_id=peer, device_id_type=MESH)
    for i in (9, 8, 7, 6, 5):
        loads[i].wait()

    slots = 4 * cap
    sub = lax.broadcasted_iota(jnp.int32, (slots, pipes), 0)
    lane = lax.broadcasted_iota(jnp.int32, (slots, pipes), 1)
    target = jnp.full((slots, pipes), -1, jnp.int32)
    for s in range(2):
        live = count_ref[0, s]
        for k in range(cap):
            own = jnp.where(k < live, pipe_ref[0, s, k], -1)
            target = jnp.where(sub == 2 * s * cap + k, own, target)
    chosen = (lane == target).astype(f32)
    sub_j = lax.broadcasted_iota(jnp.int32, (slots, juncs), 0)
    lane_j = lax.broadcasted_iota(jnp.int32, (slots, juncs), 1)
    landing_at = jnp.full((slots, juncs), -1, jnp.int32)
    for s in range(2):
        for k in range(cap):
            landing_at = jnp.where(
                sub_j == (2 * s + 1) * cap + k, arrival_ref[0, s, k], landing_at
            )
    landing = (lane_j == landing_at).astype(f32)
    interior = 1.0 - jnp.sum(chosen, axis=0, keepdims=True)
    junction = lax.broadcasted_iota(jnp.int32, (juncs, pipes), 0)
    incidence = (junction == head_ref[...]).astype(f32) * interior - (
        junction == tail_ref[...]
    ).astype(f32)
    landing16 = landing.astype(bf16)
    reach = chosen + dot(landing16, incidence.astype(bf16))

    def swapped(x):
        return jnp.concatenate(
            [
                x[cap : 2 * cap],
                x[:cap],
                x[3 * cap :],
                x[2 * cap : 3 * cap],
            ],
            axis=0,
        )

    reach_out = swapped(reach).astype(bf16)
    reach_out2 = jnp.concatenate([reach_out] * 2, axis=1)
    landing_out = swapped(landing).astype(bf16)
    pad_l = jnp.concatenate([landing, jnp.zeros((128 - slots, juncs), f32)], axis=0)
    pairs_out[...] = lax.dot_general(
        landing16,
        pad_l.astype(bf16),
        (((1,), (1,)), ((), ())),
        preferred_element_type=f32,
    )

    loads[1].wait()
    loads[2].wait()
    prior = prior_ref[...]
    prior_cut = cut2(prior)
    wanted = cut2(demand_ref[...])
    outgoing[0] = dot(reach_out2, prior_cut) - dot(
        jnp.concatenate([landing_out] * 2, axis=1), wanted
    )
    pl.semaphore_wait(barrier, nets * hours - 1)

    def remote(src, dst, send, recv, shift):
        return pltpu.make_async_remote_copy(
            src_ref=src,
            dst_ref=dst,
            send_sem=send,
            recv_sem=recv,
            device_id=(net + shift, hour),
            device_id_type=MESH,
        )

    def pair_copies():
        yield has_right, has_left, remote(
            pairs_out, pairs_in.at[0], pair_send.at[0], pair_recv.at[0], 1
        )
        yield has_left, has_right, remote(
            pairs_out, pairs_in.at[1], pair_send.at[1], pair_recv.at[1], -1
        )

    def row_copies(r):
        def one(i, start, size, dest, shift):
            return remote(
                outgoing.at[r, pl.ds(start, size)],
                incoming.at[r, pl.ds(dest, size)],
                row_send.at[r, i],
                row_recv.at[r, i],
                shift,
            )

        yield has_right, has_left, one(0, 2 * cap, 2 * cap, 0, 1)
        yield has_left, has_right, one(1, 0, 2 * cap, 2 * cap, -1)
        yield has_right2, has_left2, one(2, 3 * cap, cap, 4 * cap, 2)
        yield has_left2, has_right2, one(3, cap, cap, 5 * cap, -2)

    def start(copies):
        for sends, _, copy in copies:

            @pl.when(sends)
            def _():
                copy.start()

    def arrived(copies):
        for _, receives, copy in copies:

            @pl.when(receives)
            def _():
                copy.wait_recv()

    def left_here(copies):
        for sends, _, copy in copies:

            @pl.when(sends)
            def _():
                copy.wait_send()

    start(pair_copies())
    start(row_copies(0))
    loads[4].wait()

    spread = jnp.broadcast_to(coef_ref[...], (half, length))
    rolled = pltpu.roll(spread, 0, 1, stride=1, stride_axis=0)
    at_row = lax.broadcasted_iota(jnp.int32, (half, half), 0)
    at_col = lax.broadcasted_iota(jnp.int32, (half, half), 1)
    near = jnp.where(at_col >= at_row, rolled[:, :half], 0.0)
    far = rolled[:, half:]
    for i, block in enumerate((near, far, near.T, far.T)):
        high, low = split2(block)
        toep[i, pl.ds(0, half)] = high
        toep[i, pl.ds(half, half)] = high
        toep[i, pl.ds(2 * half, half)] = low


    def thrice(high, low, i):
        return dot(jnp.concatenate([high, low, high], axis=1), toep[i])

    def forward(high, low):
        high, low = halves(high), halves(low)
        same = thrice(high, low, 0)
        cross = thrice(high[:pipes], low[:pipes], 1)
        return jnp.concatenate([same[:pipes], same[pipes:] + cross], axis=1)

    def backward(field):
        high, low = split2(halves(field))
        same = thrice(high, low, 2)
        cross = thrice(high[pipes:], low[pipes:], 3)
        return jnp.concatenate([same[:pipes] + cross, same[pipes:]], axis=1)

    loads[3].wait()
    loads[0].wait()
    eye = lax.broadcasted_iota(jnp.int32, (pipes, pipes), 0) == (
        lax.broadcasted_iota(jnp.int32, (pipes, pipes), 1)
    )
    sigma = jnp.sum(jnp.where(eye, sigma_ref[...], 0.0), axis=1, keepdims=True)
    inverse = 1.0 / sigma
    inverse2 = inverse * inverse
    whitened = forward(*split2((measured_ref[...] - prior) * inverse))
    huber = EDGE / jnp.maximum(jnp.abs(whitened), EDGE)
    weight[...] = huber
    near_part = backward(huber * whitened * sigma) * inverse2

    arrived(pair_copies())
    zero = jnp.zeros((cap, pipes), f32)
    fill = jnp.zeros((128 - slots, pipes), f32)
    lower = chosen[:cap]
    upper = chosen[2 * cap : 3 * cap]
    lower_at = jnp.concatenate([zero, zero, zero, lower, fill], axis=0)
    upper_at = jnp.concatenate([zero, upper, zero, zero, fill], axis=0)
    from_left = dot(pairs_in[0].astype(bf16), lower_at.astype(bf16))
    from_right = dot(pairs_in[1].astype(bf16), upper_at.astype(bf16))
    gather = jnp.concatenate(
        [reach, from_left[cap : 2 * cap], from_right[3 * cap :]], axis=0
    )
    width = 6 * cap
    deep = -(-2 * width // 128) * 128
    gather2 = jnp.concatenate(
        [gather] * 2 + [jnp.zeros((deep - 2 * width, pipes), f32)], axis=0
    )
    spread_in = (PENALTY * gather2.T).astype(bf16)
    onward = dot(reach_out, spread_in).astype(bf16)
    gather_both = jnp.concatenate([PENALTY * gather] * 2, axis=1).astype(bf16)
    tall = -(-(juncs + 2 * cap) // 128) * 128
    rest = jnp.zeros((tall - juncs - 2 * cap, pipes), f32)
    left_side = jnp.concatenate([incidence, lower, upper, rest], axis=0).T
    right_side = jnp.concatenate(
        [incidence, from_left[3 * cap :], from_right[cap : 2 * cap], rest], axis=0
    )
    local = (
        PENALTY * dot(left_side.astype(bf16), right_side.astype(bf16))
    ).astype(bf16)
    local2 = jnp.concatenate([local] * 2, axis=1)
    back = (PENALTY * left_side).astype(bf16)
    empty = jnp.zeros((tall - juncs, length), bf16)
    wanted = jnp.concatenate([wanted[:juncs], empty, wanted[juncs:], empty], axis=0)
    tail_rows = jnp.zeros((deep - 2 * width, length), bf16)

    def cut_rows(x):
        return jnp.concatenate(split2(x) + (tail_rows,), axis=0)

    def received(r):
        arrived(row_copies(r))
        return cut_rows(incoming[r])

    def send(r, rows):
        outgoing[r] = rows
        start(row_copies(r))

    def near(field):
        pieces = split2(field)
        cut = jnp.concatenate(pieces, axis=0)
        here = dot(local2, cut)
        filtered = forward(*pieces)
        return here + backward(weight[...] * filtered) * inverse2, cut

    def rows_of(field):
        return dot(reach_out2, cut2(field))

    at = lax.broadcasted_iota(jnp.int32, (1, 128), 1)

    def share(i, values):
        mine = jnp.zeros((1, 128), f32)
        for k, value in enumerate(values):
            mine = jnp.where(at == k, value, mine)
        part[i] = mine
        for slot, peer in others():
            pltpu.make_async_remote_copy(
                src_ref=part.at[i],
                dst_ref=parts.at[i, slot],
                send_sem=sum_send.at[i],
                recv_sem=sum_recv.at[i],
                device_id=peer,
                device_id_type=MESH,
            ).start()

    def whole(sem, i):
        pltpu.make_async_copy(parts.at[i], parts.at[i], sem.at[i]).wait()

    def shared(i, count):
        whole(sum_recv, i)
        sums = part[i] + jnp.sum(parts[i], axis=0)
        return [sums[:, k : k + 1] for k in range(count)]

    here = near_part + dot(jnp.concatenate([back] * 2, axis=1), wanted)
    here = here - dot(local2, prior_cut)
    rows = rows_of(here)
    came = received(0)
    send(1, rows - dot(onward, came))
    start0 = here - dot(spread_in, came)
    basis[0] = start0
    square = total(start0 * start0)
    here, _ = near(start0)
    rows = rows_of(here)
    came = received(1)
    send(2, rows + dot(onward, came))
    image0 = here + dot(spread_in, came)
    share(0, [square, total(start0 * image0)])
    here, _ = near(image0)
    rows = rows_of(here)
    came = received(2)
    send(3, rows + dot(onward, came))
    image00 = here + dot(spread_in, came)
    square, curve = shared(0, 2)
    first = square / curve
    start0 = basis[0]
    after = start0 - first * image0
    image = first * (image0 - first * image00)
    basis[1] = after
    basis[2] = image
    pairs = ((start0, after), (start0, image), (after, after), (after, image), (image, image))
    known = [total(x * y) for x, y in pairs]
    here, cut = near(image)
    taken = dot(gather_both, cut)
    local_part = total(image * here)
    arrived(row_copies(3))
    came = first * (incoming[2] - first * incoming[3])
    share(1, known + [first * (local_part + total(taken * came))])
    basis[3] = first * (here + dot(spread_in, cut_rows(came)))
    for r in range(ITERS + 1):
        left_here(row_copies(r))
    left_here(pair_copies())
    whole(sum_send, 0)
    sa, si, aa, ai, ii, ij = shared(1, 6)
    sj, aj = si - ai, ii
    whole(sum_send, 1)
    gram = ((square, sa, si, sj), (sa, aa, ai, aj), (si, ai, ii, ij))

    def product(a, b):
        out = None
        for i in range(4):
            for j in range(4):
                if i < 3 or j < 3:
                    term = a[i] * b[j] * (gram[i][j] if i < 3 else gram[j][i])
                    out = term if out is None else out + term
        return out

    zero = jnp.zeros((1, 1), f32)
    one = jnp.ones((1, 1), f32)
    remaining = [zero, one, zero, zero]
    now = aa
    direction = [now / square, one, zero, zero]
    moved = [one, zero, zero, zero]
    for i in range(1, ITERS):
        applied = [direction[0], -direction[0], direction[1], direction[2]]
        step = now / product(direction, applied)
        moved = [x + step * y for x, y in zip(moved, direction)]
        remaining = [x - step * y for x, y in zip(remaining, applied)]
        if i + 1 < ITERS:
            later = product(remaining, remaining)
            direction = [x + later / now * y for x, y in zip(remaining, direction)]
            now = later
    flows, residual = prior_ref[...], remaining[3] * basis[3]
    for i in range(3):
        flows = flows + first * moved[i] * basis[i]
        residual = residual + remaining[i] * basis[i]
    flows_ref[...] = flows
    residual_ref[...] = residual


def write_out(flows_ref, residual_ref, flows_out, residual_out, done):
    copies = [
        pltpu.make_async_copy(flows_ref, flows_out, done.at[0]),
        pltpu.make_async_copy(residual_ref, residual_out, done.at[1]),
    ]
    for copy in copies:
        copy.start()
    for copy in copies:
        copy.wait()


def shards(nets, hours, *args):
    prior, demand, pipe = args[1], args[2], args[7]
    pipes, length = prior.shape
    cap = pipe.shape[2]
    args = [x.reshape(1, -1) if x.ndim == 1 else x for x in args]
    args = [pltpu.with_memory_space_constraint(x, pltpu.HBM) for x in args]
    vmem = pl.BlockSpec(memory_space=pltpu.VMEM)
    rounds = ITERS + 1
    field = jax.ShapeDtypeStruct(prior.shape, f32)
    results = pl.pallas_call(
        functools.partial(kernel, nets, hours),
        out_shape=(field, field),
        in_specs=[pl.BlockSpec(memory_space=pltpu.HBM)] * 10,
        out_specs=(vmem, vmem),
        scratch_shapes=[pltpu.VMEM(x.shape, x.dtype) for x in args[:7]]
        + [pltpu.SMEM(x.shape, x.dtype) for x in args[7:]]
        + [
            pltpu.SemaphoreType.DMA((10,)),
            pltpu.VMEM((pipes, length), f32),
            pltpu.VMEM((4, 3 * (length // 2), length // 2), bf16),
            pltpu.VMEM((rounds, 4 * cap, length), f32),
            pltpu.VMEM((rounds, 6 * cap, length), f32),
            pltpu.VMEM((4 * cap, 128), f32),
            pltpu.VMEM((2, 4 * cap, 128), f32),
            pltpu.VMEM((rounds, pipes, length), f32),
            pltpu.VMEM((2, 1, 128), f32),
            pltpu.VMEM((2, nets * hours - 1, 1, 128), f32),
            pltpu.SemaphoreType.DMA((rounds, 4)),
            pltpu.SemaphoreType.DMA((rounds, 4)),
            pltpu.SemaphoreType.DMA((2,)),
            pltpu.SemaphoreType.DMA((2,)),
            pltpu.SemaphoreType.DMA((2,)),
            pltpu.SemaphoreType.DMA((2,)),
        ],
        compiler_params=pltpu.CompilerParams(
            collective_id=0, has_side_effects=True, vmem_limit_bytes=32 * 2**20
        ),
        cost_estimate=pl.CostEstimate(
            flops=3 * 8 * 2 * pipes * length * length,
            bytes_accessed=5 * 4 * pipes * length,
            transcendentals=0,
        ),
    )(*args)
    hbm = pl.BlockSpec(memory_space=pltpu.HBM)
    return pl.pallas_call(
        write_out,
        out_shape=(field, field),
        in_specs=[vmem, vmem],
        out_specs=(hbm, hbm),
        scratch_shapes=[pltpu.SemaphoreType.DMA((2,))],
    )(*[pltpu.with_memory_space_constraint(x, pltpu.VMEM) for x in results])

def solution(mesh):
    placed = (
        P("net", "hour"),
        P("net", "hour"),
        P("net", "hour"),
        P("net"),
        P(),
        P("net"),
        P("net"),
        P("net", None, None),
        P("net", None),
        P("net", None, None),
    )
    return jax.shard_map(
        functools.partial(shards, mesh.shape["net"], mesh.shape["hour"]),
        mesh=mesh,
        in_specs=placed,
        out_specs=(P("net", "hour"), P("net", "hour")),
        check_vma=False,
    )
```
